32 devices in a mesh: gx: 2 (over y), gy: 16 (over z, x, core).
Axes of the slice: x: 2, y: 2, z: 4, core: 2. Of those that a mesh axis runs over, the one named last changes fastest.
Arguments:
- source: float32 [128, 64, 128], P('gy', 'gx'), may hold values from -0.004 to 0.004
- mask: int32 [128, 64, 128], P('gy', 'gx'), may hold values from 0 to 2, as said below
- cond_x: float32 [128, 64, 128], P('gy', 'gx'), may hold values from 0.0012 to 0.06
- cond_y: float32 [128, 64, 128], P('gy', 'gx'), may hold values from 0.4 to 5
- cond_z: float32 [128, 64, 128], P('gy', 'gx'), may hold values from 0.0004 to 0.01
Outputs:
- solution: float32 [128, 64, 128], P('gy', 'gx')
The draws below stay inside these ranges and needn't reach their ends.
Inputs may be any that keep to these rules, and one draw needn't show every extreme that they name: `mask`: 0 marks a fluid cell, 1 a cut cell, 2 a solid cell.
All inputs are finite; a program needn't handle non-finite values.
Results may differ from the reference program's by a relative error of at most 0.00095.
Values sent between devices are 32-bit elements; how exact they have to be, the bound alone decides.
A program may use at most 128 MiB of HBM per device.

```python
import math
import jax
import jax.numpy as jnp
from jax import lax

CZ = 128
LEVELS = 6
NX = 64
NY = 128


def draw_mask(key, part):
    keys = jax.random.split(key, 4)
    least = min(NY, NX, CZ)
    radius = jax.random.randint(keys[0], (), max(1, least // 8), max(2, least // 4 + 1))
    centre_y = jax.random.randint(keys[1], (), 0, NY)
    centre_x = jax.random.randint(keys[2], (), 0, NX)
    centre_z = jax.random.randint(keys[3], (), 0, CZ)
    along_y = (jnp.arange(NY, dtype=jnp.int32) - centre_y)[:, None, None]
    along_x = (jnp.arange(NX, dtype=jnp.int32) - centre_x)[None, :, None]
    along_z = (jnp.arange(CZ, dtype=jnp.int32) - centre_z)[None, None, :]
    distance = along_y * along_y + along_x * along_x + along_z * along_z
    solid = distance <= radius * radius
    shell = distance <= (radius + 2) * (radius + 2)
    return jnp.where(solid, 2, jnp.where(shell, 1, 0)).astype(jnp.int32)


def draw_source(key, part):
    keys = jax.random.split(key, 1)
    return jnp.clip(0.0008 * jax.random.normal(keys[0], (NY, NX, CZ), jnp.float32), -0.004, 0.004)


def log_between(key, lowest, highest):
    return jnp.exp(jax.random.uniform(key, (NY, NX, CZ), jnp.float32, math.log(lowest), math.log(highest)))


def coefficient(key, offset_tag, slab_depth, bounds):
    slab_start = jax.random.randint(jax.random.fold_in(key, 101), (), 0, NY - slab_depth + 1)
    row_index = jnp.arange(NY, dtype=jnp.int32)[:, None, None]
    inside = (row_index >= slab_start) & (row_index < slab_start + slab_depth)
    subkeys = jax.random.split(jax.random.fold_in(key, offset_tag), 2)
    outside_values = log_between(subkeys[0], bounds[0], bounds[1])
    inside_values = log_between(subkeys[1], bounds[2], bounds[3])
    return jnp.where(inside, inside_values, outside_values)


def draw_cond_x(key, part):
    return coefficient(key, 11, NY // 4, (0.003, 0.06, 0.003, 0.006))


def draw_cond_y(key, part):
    return coefficient(key, 12, NY // 4, (0.4, 2.5, 1.25, 2.5))


def draw_cond_z(key, part):
    return coefficient(key, 13, NY // 4, (0.001, 0.01, 0.001, 0.002))


def setup_inputs(seed: int = 0) -> dict:
    streams_of = jax.random.split(jax.random.key(seed), 6)
    return {
        "source": draw_source(jax.random.fold_in(streams_of[5], 71), 0),
        "mask": draw_mask(jax.random.fold_in(streams_of[5], 71), 0),
        "cond_x": draw_cond_x(jax.random.fold_in(streams_of[5], 71), 0),
        "cond_y": draw_cond_y(jax.random.fold_in(streams_of[5], 71), 0),
        "cond_z": draw_cond_z(jax.random.fold_in(streams_of[5], 71), 0),
    }


base_shift = 0.001
wall_term = 0.02


def ahead(field, axis):
    size = field.shape[axis]
    edge = jnp.zeros_like(lax.slice_in_dim(field, 0, 1, axis=axis))
    return jnp.concatenate([lax.slice_in_dim(field, 1, size, axis=axis), edge], axis=axis)


def behind(field, axis):
    size = field.shape[axis]
    edge = jnp.zeros_like(lax.slice_in_dim(field, 0, 1, axis=axis))
    return jnp.concatenate([edge, lax.slice_in_dim(field, 0, size - 1, axis=axis)], axis=axis)


def coarse_sum(field):
    depth, width, height = field.shape
    return field.reshape(depth // 2, 2, width // 2, 2, height // 2, 2).sum(axis=(1, 3, 5))


def coarse_face(face, axis, parity):
    picked = lax.slice_in_dim(face, parity, face.shape[axis], stride=2, axis=axis)
    return 0.125 * coarse_sum(jnp.repeat(picked, 2, axis=axis))


def prolong(field):
    return jnp.repeat(jnp.repeat(jnp.repeat(field, 2, axis=0), 2, axis=1), 2, axis=2)


def make_level(face_x, face_y, face_z, shift):
    level = {"face_x": face_x, "face_y": face_y, "face_z": face_z}
    level["low_x"] = behind(face_x, 1)
    level["low_y"] = behind(face_y, 0)
    level["low_z"] = behind(face_z, 2)
    level["diag"] = shift + face_x + level["low_x"] + face_y + level["low_y"] + face_z + level["low_z"]
    return level


def neighbour_terms(level, field):
    return (level["face_x"] * ahead(field, 1) + level["low_x"] * behind(field, 1)
            + level["face_z"] * ahead(field, 2) + level["low_z"] * behind(field, 2))


def line_solve(level, rhs):
    lower = -level["low_y"]
    upper = -level["face_y"]
    diag = level["diag"]

    def sweep(carry, row):
        ratio_prev, value_prev = carry
        below, middle, above, right = row
        pivot = middle - below * ratio_prev
        ratio = above / pivot
        value = (right - below * value_prev) / pivot
        return (ratio, value), (ratio, value)

    zero = jnp.zeros(rhs.shape[1:], jnp.float32)
    unused, (ratios, values) = lax.scan(sweep, (zero, zero), (lower, diag, upper, rhs))

    def back(after, row):
        ratio, value = row
        now = value - ratio * after
        return now, now

    unused, result = lax.scan(back, zero, (ratios, values), reverse=True)
    return result


def relax(level, field, rhs):
    if field is None:
        return line_solve(level, rhs)
    return line_solve(level, rhs + neighbour_terms(level, field))


def residual_of(level, field, rhs):
    applied = (level["diag"] * field - level["face_y"] * ahead(field, 0)
               - level["low_y"] * behind(field, 0) - neighbour_terms(level, field))
    return rhs - applied


def cycle(levels, depth, rhs):
    level = levels[depth]
    field = relax(level, None, rhs)
    if depth == len(levels) - 1:
        return relax(level, field, rhs)
    residual = residual_of(level, field, rhs)
    correction = cycle(levels, depth + 1, 0.25 * coarse_sum(residual))
    field = field + prolong(correction)
    return relax(level, field, rhs)


def reference(source, mask, cond_x, cond_y, cond_z):
    open_cells = (mask != 2).astype(jnp.float32)
    wall = (mask == 1).astype(jnp.float32)
    face_x = cond_x * open_cells * ahead(open_cells, 1)
    face_y = cond_y * open_cells * ahead(open_cells, 0)
    face_z = cond_z * open_cells * ahead(open_cells, 2)
    shift = base_shift + wall_term * wall
    levels = [make_level(face_x, face_y, face_z, shift)]
    for depth in range(1, LEVELS):
        face_x = coarse_face(face_x, 1, 1)
        face_y = coarse_face(face_y, 0, 1)
        face_z = coarse_face(face_z, 2, 1)
        shift = 0.25 * coarse_sum(shift)
        levels.append(make_level(face_x, face_y, face_z, shift))
    return cycle(levels, 0, source * open_cells)
```

```python
import functools

import jax
import jax.numpy as jnp
from jax import lax
from jax.experimental import pallas as pl
from jax.experimental.pallas import tpu as pltpu
from jax.sharding import PartitionSpec as P

LEVELS = 6


base_shift = 0.001
wall_term = 0.02


def padded(cells, sides, width):
    for axis, dim in sides:
        count = lax.axis_size(axis)
        ends = count - 1
        head = lax.slice_in_dim(cells, 0, width, axis=dim)
        tail = lax.slice_in_dim(cells, cells.shape[dim] - width, cells.shape[dim], axis=dim)
        cells = jnp.concatenate(
            [
                lax.ppermute(tail, axis, [(i, (i + 1) % count) for i in range(ends)]),
                cells,
                lax.ppermute(head, axis, [((i + 1) % count, i) for i in range(ends)]),
            ],
            axis=dim,
        )
    return cells


def swapped(x, axis, stride):
    return lax.ppermute(x, axis, [(i, i ^ 1 << stride) for i in range(lax.axis_size(axis))])


def ahead(field, axis):
    size = field.shape[axis]
    edge = jnp.zeros_like(lax.slice_in_dim(field, 0, 1, axis=axis))
    return jnp.concatenate([lax.slice_in_dim(field, 1, size, axis=axis), edge], axis=axis)


def behind(field, axis):
    size = field.shape[axis]
    edge = jnp.zeros_like(lax.slice_in_dim(field, 0, 1, axis=axis))
    return jnp.concatenate([edge, lax.slice_in_dim(field, 0, size - 1, axis=axis)], axis=axis)


def coarse_sum(field):
    depth, width, height = field.shape
    return field.reshape(depth // 2, 2, width // 2, 2, height // 2, 2).sum(axis=(1, 3, 5))


def coarse_face(face, axis, parity):
    picked = lax.slice_in_dim(face, parity, face.shape[axis], stride=2, axis=axis)
    return 0.125 * coarse_sum(jnp.repeat(picked, 2, axis=axis))


def prolong(field):
    return jnp.repeat(jnp.repeat(jnp.repeat(field, 2, axis=0), 2, axis=1), 2, axis=2)


def upper_flag(bit):
    return lax.axis_index("gy") // 2**bit % 2


def line_factors(lower, diag, upper):
    denoms = [diag[0]]
    ratios = [upper[0] / diag[0]]
    for place in range(1, diag.shape[0]):
        pivot = diag[place] - lower[place] * ratios[place - 1]
        denoms.append(pivot)
        ratios.append(upper[place] / pivot)
    return (denoms, ratios)


def rows_solve(level, rhs):
    lower = level["lower"]
    denoms = level["denoms"]
    ratios = level["ratios"]
    count = rhs.shape[0]
    values = [rhs[0] / denoms[0]]
    for place in range(1, count):
        values.append((rhs[place] - lower[place] * values[place - 1]) / denoms[place])
    result = [values[count - 1]]
    for place in range(count - 2, -1, -1):
        result.append(values[place] - ratios[place] * result[-1])
    return jnp.stack(result[::-1])


def assemble(faces, group):
    face_x, low_x, face_y, low_y, face_z, shift = faces
    low_z = behind(face_z, 2)
    diag = shift + face_x + low_x + face_y + low_y + face_z + low_z
    level = {
        "face_x": face_x,
        "low_x": low_x,
        "face_y": face_y,
        "low_y": low_y,
        "face_z": face_z,
        "low_z": low_z,
        "diag": diag,
        "group": group,
    }
    level["lower"] = -low_y
    denoms, ratios = line_factors(-low_y, diag, -face_y)
    level["denoms"] = denoms
    level["ratios"] = ratios
    blank = jnp.zeros_like(diag)
    level["first_resp"] = rows_solve(level, blank.at[0].set(1.0))
    level["last_resp"] = rows_solve(level, blank.at[-1].set(1.0))
    level["alpha"] = low_y[0] * level["first_resp"][0]
    level["gamma"] = low_y[0] * level["first_resp"][-1]
    level["beta"] = face_y[-1] * level["last_resp"][0]
    level["delta"] = face_y[-1] * level["last_resp"][-1]
    return level


def forward_terms(alpha, beta, gamma, delta, head, tail):
    zeros = jnp.zeros_like(head)
    ones = jnp.ones_like(head)
    return (
        gamma * beta - alpha * delta,
        zeros,
        delta,
        gamma * head - alpha * tail,
        gamma,
        tail,
        -alpha,
        zeros,
        ones,
    )


def chain_forward(earlier, later):
    product = []
    for left_row in range(3):
        for column in range(3):
            product.append(
                later[3 * left_row] * earlier[column]
                + later[3 * left_row + 1] * earlier[3 + column]
                + later[3 * left_row + 2] * earlier[6 + column]
            )
    scale = product[8]
    return tuple((entry / scale for entry in product))


def chain_backward(earlier, later):
    return (later[0] + later[1] * earlier[0], later[1] * earlier[1])


def settle(alpha, beta, head, state):
    carry_q = state[2] / state[8]
    carry_p = state[5] / state[8]
    pivot = 1.0 - alpha * carry_q
    return ((head + alpha * carry_p) / pivot, beta / pivot, carry_q, carry_p)


def reduced_local(alpha, beta, gamma, delta, head, tail):
    zeros = jnp.zeros_like(head[:1])
    ones = jnp.ones_like(head[:1])
    identity = (ones, zeros, zeros, zeros, ones, zeros, zeros, zeros, ones)
    terms = forward_terms(alpha, beta, gamma, delta, head, tail)
    inclusive = lax.associative_scan(chain_forward, terms, axis=0)
    state = tuple(
        (jnp.concatenate([plain, entry[:-1]], axis=0) for plain, entry in zip(identity, inclusive))
    )
    start, slope, carry_q, carry_p = settle(alpha, beta, head, state)
    later = lax.associative_scan(chain_backward, (start, slope), reverse=True, axis=0)
    next_first = jnp.concatenate([later[0][1:], zeros], axis=0)
    first = start + slope * next_first
    return (carry_p + carry_q * first, next_first)


def pick_block(values, index, shape):
    return lax.dynamic_index_in_dim(values, index, 0, keepdims=False).reshape(shape)


def reduced_moved(level, head, tail):
    group = level["group"]
    shape = head.shape
    packed = jnp.stack(
        [level["alpha"], level["beta"], level["gamma"], level["delta"], head, tail]
    ).reshape(6, 1, -1)
    if group == 1:
        moved = lax.all_to_all(packed, "gy", split_axis=2, concat_axis=1, tiled=True)
        prev_last, next_first = reduced_local(
            moved[0], moved[1], moved[2], moved[3], moved[4], moved[5]
        )
        back = lax.all_to_all(
            jnp.stack([prev_last, next_first]), "gy", split_axis=1, concat_axis=2, tiled=True
        )
        return (back[0, 0].reshape(shape), back[1, 0].reshape(shape))
    whole = lax.all_gather(packed, "gy", axis=1, tiled=True)
    whole = whole.reshape(6, whole.shape[1] // group, group, -1)[:, :, 0]
    prev_last, next_first = reduced_local(
        whole[0], whole[1], whole[2], whole[3], whole[4], whole[5]
    )
    index = lax.axis_index("gy") // group
    return (pick_block(prev_last, index, shape), pick_block(next_first, index, shape))


def line_solve(level, rhs):
    local = rows_solve(level, rhs)
    prev_last, next_first = reduced_moved(level, local[0], local[-1])
    return (
        local
        + (level["low_y"][0] * prev_last)[None] * level["first_resp"]
        + (level["face_y"][-1] * next_first)[None] * level["last_resp"]
    )


def neighbour_terms(level, field):
    rim = padded(field, (("gx", 1),), 1)
    return (
        level["face_x"] * rim[:, 2:]
        + level["low_x"] * rim[:, :-2]
        + level["face_z"] * ahead(field, 2)
        + level["low_z"] * behind(field, 2)
    )


def relax(level, field, rhs):
    return line_solve(level, rhs + neighbour_terms(level, field))


def body(source, mask, cond_x, cond_y, cond_z):
    open_cells = (mask != 2).astype(jnp.float32)
    wall = (mask == 1).astype(jnp.float32)
    rim = padded(
        jnp.stack([cond_x * open_cells, cond_y * open_cells, open_cells]), (("gx", 2), ("gy", 1)), 1
    )
    faces = (
        cond_x * open_cells * rim[2, 1:-1, 2:],
        rim[0, 1:-1, :-2] * open_cells,
        cond_y * open_cells * rim[2, 2:, 1:-1],
        rim[1, :-2, 1:-1] * open_cells,
        cond_z * open_cells * ahead(open_cells, 2),
        base_shift + wall_term * wall,
    )
    rhs = source * open_cells
    levels = []
    fields = []
    sources = []
    residual = rhs
    for depth in range(LEVELS):
        group = 1
        if depth > 0:
            face_x, low_x, face_y, low_y, face_z, shift = faces
            faces = (
                coarse_face(face_x, 1, 1),
                coarse_face(low_x, 1, 0),
                coarse_face(face_y, 0, 1),
                coarse_face(low_y, 0, 0),
                coarse_face(face_z, 2, 1),
                0.25 * coarse_sum(shift),
            )
            rhs = 0.25 * coarse_sum(residual)
            if depth >= 2:
                group = 2 ** (depth - 1)
                stacked = jnp.stack((rhs,) + faces)
                partner = swapped(stacked, "gy", depth - 2)
                upper = upper_flag(depth - 2) == 1
                folded = jnp.concatenate(
                    [jnp.where(upper, partner, stacked), jnp.where(upper, stacked, partner)], axis=1
                )
                rhs = folded[0]
                faces = tuple((folded[place] for place in range(1, 7)))
        level = assemble(faces, group)
        field = line_solve(level, rhs)
        if depth == LEVELS - 1:
            field = relax(level, field, rhs)
        else:
            residual = neighbour_terms(level, field)
        levels.append(level)
        fields.append(field)
        sources.append(rhs)
    correction = fields[-1]
    for depth in range(LEVELS - 2, -1, -1):
        if depth + 1 >= 2:
            half = correction.shape[0] // 2
            correction = lax.dynamic_slice_in_dim(correction, upper_flag(depth - 1) * half, half, 0)
        field = fields[depth] + prolong(correction)
        correction = relax(levels[depth], field, sources[depth])
    return correction

MESH = pl.DeviceIdType.MESH
LANES = 128
EXACT = lax.Precision.HIGHEST


def looped(count, step, carry, unroll=4):
    while count % unroll:
        unroll //= 2

    def several(outer, carry):
        for inner in range(unroll):
            carry = step(outer * unroll + inner, carry)
        return carry

    return lax.fori_loop(0, count // unroll, several, carry)


def pairing(parity):
    fine = lax.broadcasted_iota(jnp.int32, (LANES, LANES), 0)
    coarse = lax.broadcasted_iota(jnp.int32, (LANES, LANES), 1)
    if parity is None:
        hit = (fine == 2 * coarse) | (fine == 2 * coarse + 1)
    else:
        hit = fine == 2 * coarse + parity
    return jnp.where(hit, 1.0, 0.0).astype(jnp.float32)


def spreading():
    coarse = lax.broadcasted_iota(jnp.int32, (LANES, LANES), 0)
    fine = lax.broadcasted_iota(jnp.int32, (LANES, LANES), 1)
    hit = (fine == 2 * coarse) | (fine == 2 * coarse + 1)
    return jnp.where(hit, 1.0, 0.0).astype(jnp.float32)


def times(left, right):
    return jnp.dot(left, right, precision=EXACT, preferred_element_type=jnp.float32)


def coarsened(field, work, y_odd=False, x_odd=False, z_odd=False):
    rows, wide, lanes = field.shape
    pairs = field.reshape(rows // 2, 2, wide, lanes)
    summed = pairs[:, 1] if y_odd else pairs[:, 0] + pairs[:, 1]
    count = rows // 2 * wide
    work[pl.ds(0, count), :] = times(summed.reshape(count, lanes), pairing(1 if z_odd else None))
    result = work[pl.ds(1, count // 2, stride=2), :]
    if not x_odd:
        result = result + work[pl.ds(0, count // 2, stride=2), :]
    return 0.25 * result


def put_rows(target, flat, rows):
    wide = flat.shape[0] // rows
    if wide % 8 == 0:
        target[...] = flat.reshape(rows, wide, LANES)
        return
    target[...] = jnp.zeros_like(target)
    for row in range(rows):
        target[row, pl.ds(0, wide), :] = flat[row * wide : (row + 1) * wide]


def spread_add(target, coarse, wide, work):
    rows = coarse.shape[0]
    half = coarse.shape[1]
    flat = times(coarse.reshape(rows * half, LANES), spreading())
    work[pl.ds(0, rows * half, stride=2), :] = flat
    work[pl.ds(1, rows * half, stride=2), :] = flat
    for row in range(rows):
        extra = work[pl.ds(row * 2 * half, wide), :]
        target[2 * row] = target[2 * row] + extra
        target[2 * row + 1] = target[2 * row + 1] + extra


class Coarse:
    names = ("fx", "lx", "fy", "ly", "fz", "lz", "sh", "rec", "u", "g")

    def __init__(self, rows, width, height):
        self.rows = rows
        self.width = width
        self.height = height
        self.wide = max(8, width)

    def scratch(self):
        return [pltpu.VMEM((self.rows, self.wide, LANES), jnp.float32)] * len(self.names)

    def bind(self, refs):
        for name, ref in zip(self.names, refs):
            setattr(self, name, ref)
        self.halo = None

    def factor(self, edge=None):
        row = lax.broadcasted_iota(jnp.int32, (self.wide, LANES), 0)
        lane = lax.broadcasted_iota(jnp.int32, (self.wide, LANES), 1)
        blank = jnp.where((row >= self.width) | (lane >= self.height), 1.0, 0.0)
        zero = jnp.zeros((self.wide, LANES), jnp.float32)

        def step(y, carry):
            ratio, below = carry
            fx, fy, fz = self.fx[y], self.fy[y], self.fz[y]
            lx = pltpu.roll(fx, 1, 0)
            if edge is not None:
                lx = jnp.where(row == 0, edge(y), lx)
            lz = pltpu.roll(fz, 1, 1)
            diag = self.sh[y] + blank + fx + lx + fy + below + fz + lz
            rec = 1.0 / (diag - below * ratio)
            self.lx[y] = lx
            self.ly[y] = below * rec
            self.lz[y] = lz
            self.rec[y] = rec
            ratio = fy * rec
            self.sh[y] = ratio
            return ratio, fy

        looped(self.rows, step, (zero, zero))

    def beside(self, y):
        u = self.u[y]
        after = pltpu.roll(u, self.wide - 1, 0)
        before = pltpu.roll(u, 1, 0)
        if self.halo is not None:
            row = lax.broadcasted_iota(jnp.int32, (self.wide, LANES), 0)
            before = jnp.where(row == 0, self.halo[0, pl.ds(y, 1), :], before)
            after = jnp.where(row == self.wide - 1, self.halo[1, pl.ds(y, 1), :], after)
        return (
            self.fx[y] * after
            + self.lx[y] * before
            + self.fz[y] * pltpu.roll(u, LANES - 1, 1)
            + self.lz[y] * pltpu.roll(u, 1, 1)
        )

    def solve(self, again):
        zero = jnp.zeros((self.wide, LANES), jnp.float32)

        def down(y, carry):
            right = self.g[y]
            if again:
                right = right + self.beside(y)
            value = right * self.rec[y] + self.ly[y] * carry
            self.u[y] = value
            return value

        def up(step, carry):
            y = self.rows - 1 - step
            value = self.u[y] + self.sh[y] * carry
            self.u[y] = value
            return value

        looped(self.rows, down, zero, 8)
        looped(self.rows, up, zero, 8)

    def residual(self, hold):
        def step(y, carry):
            hold[y] = self.beside(y)
            return carry

        looped(self.rows, step, 0)


def v_cycle_kernel(ngx, ngy, levels, *refs):
    source, mask, cond_x, cond_y, cond_z, out = refs[:6]
    refs = list(refs[6:])

    def take(count):
        got = refs[:count]
        del refs[:count]
        return got

    rows, wide, lanes = source.shape
    gx = lax.axis_index("gx")
    gy = lax.axis_index("gy")
    (work, hold) = take(2)
    one = dict(zip(("fx", "lx", "fz", "lz", "rec", "lr", "rat", "first", "last", "f", "u"), take(11)))
    (edge_fy, edge_ly) = take(2)
    (sx, rx, sy, ry) = take(4)
    (coef_s, coef_r, rhs_s, rhs_r) = take(4)
    (face_s, face_r, back_s, back_r, face2_s, face2_r, back2_s, back2_r) = take(8)
    (red, terms, whole_prev, whole_next) = take(4)
    (xu_s, xu_r, xv_s, xv_r, h2_s, h2_r, h3_s, h3_r) = take(8)
    (c3_s, c3_r, g3_s, g3_r) = take(4)
    for level in levels:
        level.bind(take(len(Coarse.names)))
    (near_send, near_recv, all_send, all_recv, side_send, side_recv) = take(6)

    def far(src, dst, send, recv, device):
        return pltpu.make_async_remote_copy(
            src_ref=src, dst_ref=dst, send_sem=send, recv_sem=recv, device_id=device, device_id_type=MESH
        )

    def beside_copies(src, dst, slot, axis):
        place, count = (gx, ngx) if axis == 0 else (gy, ngy)
        higher = (gx + 1, gy) if axis == 0 else (gx, gy + 1)
        lower = (gx - 1, gy) if axis == 0 else (gx, gy - 1)
        up = far(src.at[0], dst.at[0], near_send.at[slot, 0], near_recv.at[slot, 0], higher)
        down = far(src.at[1], dst.at[1], near_send.at[slot, 1], near_recv.at[slot, 1], lower)
        return place, count, up, down

    def beside_start(src, dst, slot, axis):
        place, count, up, down = beside_copies(src, dst, slot, axis)

        @pl.when(place < count - 1)
        def _():
            up.start()

        @pl.when(place > 0)
        def _():
            down.start()

    def beside_wait(src, dst, slot, axis):
        place, count, up, down = beside_copies(src, dst, slot, axis)

        @pl.when(place < count - 1)
        def _():
            up.wait_send()
            down.wait_recv()

        @pl.when(place > 0)
        def _():
            down.wait_send()
            up.wait_recv()

    def all_start(src, dst, slot):
        def step(j, carry):
            peer = lax.rem(gy + j, ngy)
            far(src(peer), dst.at[gy], all_send.at[slot, peer], all_recv.at[slot, gy], (gx, peer)).start()
            return carry

        lax.fori_loop(1, ngy, step, 0)

    def all_wait(src, dst, slot):
        def step(j, carry):
            peer = lax.rem(gy + j, ngy)
            far(src(peer), dst.at[peer], all_send.at[slot, peer], all_recv.at[slot, peer], (gx, peer)).wait()
            return carry

        lax.fori_loop(1, ngy, step, 0)

    def side_start(src, dst, slot):
        for j in range(1, ngx):
            peer = lax.rem(gx + j, ngx)
            far(src, dst.at[gx], side_send.at[slot, j], side_recv.at[slot, gx], (peer, gy)).start()

    def side_wait(src, dst, slot):
        for j in range(1, ngx):
            peer = lax.rem(gx + j, ngx)
            far(src, dst.at[peer], side_send.at[slot, j], side_recv.at[slot, peer], (peer, gy)).wait()

    for ref in (rx, ry, xu_r, xv_r, h2_r, h3_r):
        ref[...] = jnp.zeros_like(ref)
    barrier = pltpu.get_barrier_semaphore()

    def greet(j, carry):
        pl.semaphore_signal(barrier, inc=1, device_id=(gx, lax.rem(gy + j, ngy)), device_id_type=MESH)
        return carry

    lax.fori_loop(1, ngy, greet, 0)
    for j in range(1, ngx):
        pl.semaphore_signal(barrier, inc=1, device_id=(lax.rem(gx + j, ngx), gy), device_id_type=MESH)
    pl.semaphore_wait(barrier, ngy - 1 + ngx - 1)

    row = lax.broadcasted_iota(jnp.int32, (wide, lanes), 0)
    lane = lax.broadcasted_iota(jnp.int32, (wide, lanes), 1)
    opened = [jnp.where(mask[y] != 2, 1.0, 0.0) for y in range(rows)]
    for y in range(rows):
        sx[0, pl.ds(y, 1), :] = (cond_x[y] * opened[y])[wide - 1 :]
        sx[1, pl.ds(y, 1), :] = opened[y][:1]
    sy[0] = cond_y[rows - 1] * opened[rows - 1]
    sy[1] = opened[0]
    beside_start(sx, rx, 0, 0)
    beside_start(sy, ry, 1, 1)
    beside_wait(sx, rx, 0, 0)
    beside_wait(sy, ry, 1, 1)
    faces_y = []
    lows_y = [ry[0] * opened[0]]
    shifts = []
    for y in range(rows):
        now = opened[y]
        cx = cond_x[y] * now
        one["fx"][y] = cx * jnp.where(row == wide - 1, rx[1, pl.ds(y, 1), :], pltpu.roll(now, wide - 1, 0))
        one["lx"][y] = now * jnp.where(row == 0, rx[0, pl.ds(y, 1), :], pltpu.roll(cx, 1, 0))
        above = opened[y + 1] if y + 1 < rows else ry[1]
        faces_y.append(cond_y[y] * now * above)
        if y + 1 < rows:
            lows_y.append(faces_y[y])
        fz = cond_z[y] * now * jnp.where(lane == lanes - 1, 0.0, pltpu.roll(now, lanes - 1, 1))
        one["fz"][y] = fz
        one["lz"][y] = pltpu.roll(fz, 1, 1)
        shifts.append(base_shift + wall_term * jnp.where(mask[y] == 1, 1.0, 0.0))
        one["f"][y] = source[y] * now
    edge_fy[...] = faces_y[rows - 1]
    edge_ly[...] = lows_y[0]

    half = rows // 2
    quarter = rows // 4
    wide2 = wide // 2
    both = lanes // 2

    def packed(flat):
        whole = flat.reshape(half, wide2, lanes)
        return whole[:quarter] + pltpu.roll(whole[quarter:], both, 2)

    coarse_fx = coarsened(one["fx"][...], work, x_odd=True)
    coef_s[pl.ds(0, quarter)] = packed(coarse_fx)
    coef_s[pl.ds(quarter, quarter)] = packed(coarsened(jnp.stack(faces_y), work, y_odd=True))
    coef_s[pl.ds(2 * quarter, quarter)] = packed(coarsened(one["fz"][...], work, z_odd=True))
    coef_s[pl.ds(3 * quarter, quarter)] = packed(coarsened(jnp.stack(shifts), work))
    lx_all = one["lx"][...].reshape(half, 2, wide, lanes)
    lx_rows = (lx_all[:, 0] + lx_all[:, 1]).reshape(half * wide, lanes)
    work[pl.ds(0, half * wide), :] = times(lx_rows, pairing(None))
    for y in range(half):
        coef_s[4 * quarter, pl.ds(y, 1), :] = 0.25 * work[pl.ds(y * wide, 1), :]
    coef_r[gy] = coef_s[...]
    all_start(lambda peer: coef_s, coef_r, 0)

    recs = []
    ratio = None
    for y in range(rows):
        diag = shifts[y] + one["fx"][y] + one["lx"][y] + faces_y[y] + lows_y[y] + one["fz"][y] + one["lz"][y]
        if y:
            diag = diag - lows_y[y] * ratio
        rec = 1.0 / diag
        ratio = faces_y[y] * rec
        recs.append(rec)
        one["rec"][y] = rec
        one["rat"][y] = ratio
        one["lr"][y] = lows_y[y] * rec

    def block_solve(right):
        value = right[0] * one["rec"][0]
        values = [value]
        for y in range(1, rows):
            value = right[y] * one["rec"][y] + one["lr"][y] * value
            values.append(value)
        for y in range(rows - 2, -1, -1):
            values[y] = values[y] + one["rat"][y] * values[y + 1]
        return values

    firsts = [recs[0]]
    for y in range(1, rows):
        firsts.append(one["lr"][y] * firsts[-1])
    lasts = [None] * (rows - 1) + [recs[rows - 1]]
    for y in range(rows - 2, -1, -1):
        firsts[y] = firsts[y] + one["rat"][y] * firsts[y + 1]
        lasts[y] = one["rat"][y] * lasts[y + 1]
    low, high = edge_ly[...], edge_fy[...]
    for y in range(rows):
        firsts[y] = low * firsts[y]
        lasts[y] = high * lasts[y]
        one["first"][y] = firsts[y]
        one["last"][y] = lasts[y]
    share = wide // ngy

    def shared(target, values):
        for place, value in enumerate(values):
            for owner in range(ngy):
                target[owner, place] = value[owner * share : (owner + 1) * share]

    def reduced(rhs, send):
        zero = jnp.zeros((share, lanes), jnp.float32)

        def down(k, carry):
            p = carry
            start = (rhs[k, 0] + face_r[k, 0] * p) * red[k, 1]
            terms[k, 0] = start
            terms[k, 1] = p
            return rhs[k, 1] + face_r[k, 2] * (p + red[k, 0] * start)

        def up(step, after):
            k = ngy - 1 - step
            first = terms[k, 0] + red[k, 2] * after
            send[k, 0] = terms[k, 1] + red[k, 0] * first
            send[k, 1] = after
            return first

        looped(ngy, down, zero)
        looped(ngy, up, zero)

    def reduced_factor():
        def step(k, q):
            inv = 1.0 / (1.0 - face_r[k, 0] * q)
            slope = face_r[k, 1] * inv
            red[k, 0] = q
            red[k, 1] = inv
            red[k, 2] = slope
            return face_r[k, 3] + face_r[k, 2] * q * slope

        looped(ngy, step, jnp.zeros((share, lanes), jnp.float32))

    def joined(local, got):
        for owner in range(ngy):
            whole_prev[pl.ds(owner * share, share), :] = got[owner, 0]
            whole_next[pl.ds(owner * share, share), :] = got[owner, 1]
        prev, after = whole_prev[...], whole_next[...]
        return [local[y] + prev * one["first"][y] + after * one["last"][y] for y in range(rows)]

    local = block_solve([one["f"][y] for y in range(rows)])
    shared(face_s, [firsts[0], lasts[0], firsts[rows - 1], lasts[rows - 1], local[0], local[rows - 1]])
    face_r[gy] = face_s[gy]
    all_start(lambda peer: face_s.at[peer], face_r, 1)
    all_wait(lambda peer: face_s.at[peer], face_r, 1)
    reduced_factor()
    reduced(face_r.at[:, pl.ds(4, 2)], back_s)
    back_r[gy] = back_s[gy]
    all_start(lambda peer: back_s.at[peer], back_r, 2)
    all_wait(lambda peer: back_s.at[peer], back_r, 2)
    values = joined(local, back_r)

    def outer_planes(values, target):
        for y in range(rows):
            target[0, pl.ds(y, 1), :] = values[y][wide - 1 :]
            target[1, pl.ds(y, 1), :] = values[y][:1]

    def beside_one(y, u, got):
        return (
            one["fx"][y] * jnp.where(row == wide - 1, got[1, pl.ds(y, 1), :], pltpu.roll(u, wide - 1, 0))
            + one["lx"][y] * jnp.where(row == 0, got[0, pl.ds(y, 1), :], pltpu.roll(u, 1, 0))
            + one["fz"][y] * pltpu.roll(u, lanes - 1, 1)
            + one["lz"][y] * pltpu.roll(u, 1, 1)
        )

    outer_planes(values, xu_s)
    beside_start(xu_s, xu_r, 2, 0)
    for y in range(rows):
        one["u"][y] = values[y]
    beside_wait(xu_s, xu_r, 2, 0)
    left = jnp.stack([beside_one(y, values[y], xu_r) for y in range(rows)])
    rhs_s[...] = packed(coarsened(left, work))
    rhs_r[gy] = rhs_s[...]
    all_start(lambda peer: rhs_s, rhs_r, 3)

    two, three = levels[0], levels[1]
    used = lax.broadcasted_iota(jnp.int32, (wide2, lanes), 1) < both

    def unpack2(target, block, k):
        for y in range(quarter):
            pair = block(y)
            target[half * k + y] = jnp.where(used, pair, 0.0)
            target[half * k + quarter + y] = jnp.where(used, pltpu.roll(pair, both, 1), 0.0)

    all_wait(lambda peer: coef_s, coef_r, 0)

    def take_coefs(k, carry):
        for place, target in enumerate((two.fx, two.fy, two.fz, two.sh)):
            unpack2(target, lambda y: coef_r[k, place * quarter + y], k)
        return carry

    lax.fori_loop(0, ngy, take_coefs, 0)

    rows3 = three.rows
    part3 = rows3 // 4
    wide3 = wide2 // 2
    step3 = lanes // 4

    def packed3(flat):
        whole = flat.reshape(rows3, wide3, lanes)
        total = whole[:part3]
        for j in range(1, 4):
            total = total + pltpu.roll(whole[j * part3 : (j + 1) * part3], j * step3, 2)
        return total

    used3 = lax.broadcasted_iota(jnp.int32, (part3, wide3, lanes), 2) < step3

    def unpack3(target, got):
        for g in range(ngx):
            block = got(g)
            for j in range(4):
                turned = block if j == 0 else pltpu.roll(block, lanes - j * step3, 2)
                target[pl.ds(j * part3, part3), pl.ds(g * wide3, wide3), :] = jnp.where(used3, turned, 0.0)

    c3_s[0] = packed3(coarsened(two.fx[...], work, x_odd=True))
    c3_s[1] = packed3(coarsened(two.fy[...], work, y_odd=True))
    c3_s[2] = packed3(coarsened(two.fz[...], work, z_odd=True))
    c3_s[3] = packed3(coarsened(two.sh[...], work))
    c3_r[gx] = c3_s[...]
    side_start(c3_s, c3_r, 0)

    def edge2(y):
        return h2_s[0, pl.ds(y, 1), :]

    def take_edges(k, carry):
        for y in range(half):
            h2_s[0, pl.ds(half * k + y, 1), :] = coef_r[k, 4 * quarter, pl.ds(y, 1), :]
        return carry

    lax.fori_loop(0, ngy, take_edges, 0)
    two.factor(edge2)
    all_wait(lambda peer: rhs_s, rhs_r, 3)

    def take_rhs(k, carry):
        unpack2(two.g, lambda y: rhs_r[k, y], k)
        return carry

    lax.fori_loop(0, ngy, take_rhs, 0)
    two.solve(False)

    def outer_two(target):
        def step(y, carry):
            target[0, pl.ds(y, 1), :] = two.u[y, pl.ds(wide2 - 1, 1), :]
            target[1, pl.ds(y, 1), :] = two.u[y, pl.ds(0, 1), :]
            return carry

        looped(two.rows, step, 0)

    outer_two(h2_s)
    beside_start(h2_s, h2_r, 3, 0)
    side_wait(c3_s, c3_r, 0)
    for place, target in enumerate((three.fx, three.fy, three.fz, three.sh)):
        unpack3(target, lambda g: c3_r[g, place])
    for fine, level in zip(levels[1:], levels[2:]):
        put_rows(level.fx, coarsened(fine.fx[...], work, x_odd=True), level.rows)
        put_rows(level.fy, coarsened(fine.fy[...], work, y_odd=True), level.rows)
        put_rows(level.fz, coarsened(fine.fz[...], work, z_odd=True), level.rows)
        put_rows(level.sh, coarsened(fine.sh[...], work), level.rows)
    for level in levels[1:]:
        level.factor()
    beside_wait(h2_s, h2_r, 3, 0)
    two.halo = h2_r
    two.residual(hold)
    g3_s[...] = packed3(coarsened(hold[...], work))
    g3_r[gx] = g3_s[...]
    side_start(g3_s, g3_r, 1)
    side_wait(g3_s, g3_r, 1)
    unpack3(three.g, lambda g: g3_r[g])
    for fine, level in zip(levels[1:], levels[2:]):
        fine.solve(False)
        part = hold.at[pl.ds(0, fine.rows), pl.ds(0, fine.wide)]
        fine.residual(part)
        put_rows(level.g, coarsened(part[...], work), level.rows)
    levels[-1].solve(False)
    levels[-1].solve(True)
    for fine, level in zip(levels[-2:0:-1], levels[:1:-1]):
        spread_add(fine.u, level.u[...], fine.wide, work)
        fine.solve(True)
    spread_add(two.u, three.u[:, pl.ds(pl.multiple_of(gx * wide3, 8), wide3), :], wide2, work)
    outer_two(h3_s)
    beside_start(h3_s, h3_r, 4, 0)
    beside_wait(h3_s, h3_r, 4, 0)
    two.halo = h3_r
    two.solve(True)
    spread_add(one["u"], two.u[pl.ds(gy * half, half)], wide, work)
    values = [one["u"][y] for y in range(rows)]
    outer_planes(values, xv_s)
    beside_start(xv_s, xv_r, 5, 0)
    beside_wait(xv_s, xv_r, 5, 0)
    local = block_solve([one["f"][y] + beside_one(y, values[y], xv_r) for y in range(rows)])
    shared(face2_s, [local[0], local[rows - 1]])
    face2_r[gy] = face2_s[gy]
    all_start(lambda peer: face2_s.at[peer], face2_r, 4)
    all_wait(lambda peer: face2_s.at[peer], face2_r, 4)
    reduced(face2_r, back2_s)
    back2_r[gy] = back2_s[gy]
    all_start(lambda peer: back2_s.at[peer], back2_r, 5)
    all_wait(lambda peer: back2_s.at[peer], back2_r, 5)
    values = joined(local, back2_r)
    for y in range(rows):
        out[y] = values[y]


def fused(ngx, ngy, *args):
    rows, wide, lanes = args[0].shape
    f32 = jnp.float32
    levels = [Coarse(rows // 2 * ngy, wide // 2, lanes // 2)]
    for depth in range(2, LEVELS):
        whole = wide * ngx >> depth
        levels.append(Coarse(rows * ngy >> depth, whole, lanes >> depth))
    two, three = levels[:2]
    share = wide // ngy
    quarter = rows // 4
    wide2 = wide // 2

    def room(*shape):
        return pltpu.VMEM(shape, f32)

    part3 = three.rows // 4
    wide3 = wide2 // 2
    most = max(rows * wide, two.rows * two.wide, three.rows * three.wide)
    scratch = [room(most, lanes), room(two.rows, two.wide, lanes)]
    scratch += [room(rows, wide, lanes)] * 11
    scratch += [room(wide, lanes)] * 2
    scratch += [room(2, rows, lanes)] * 2 + [room(2, wide, lanes)] * 2
    count = 4 * quarter + 1
    scratch += [room(count, wide2, lanes), room(ngy, count, wide2, lanes)]
    scratch += [room(quarter, wide2, lanes), room(ngy, quarter, wide2, lanes)]
    scratch += [room(ngy, 6, share, lanes)] * 2 + [room(ngy, 2, share, lanes)] * 6
    scratch += [room(ngy, 3, share, lanes), room(ngy, 2, share, lanes)]
    scratch += [room(wide, lanes)] * 2
    scratch += [room(2, rows, lanes)] * 4 + [room(2, two.rows, lanes)] * 4
    scratch += [room(4, part3, wide3, lanes), room(ngx, 4, part3, wide3, lanes)]
    scratch += [room(part3, wide3, lanes), room(ngx, part3, wide3, lanes)]
    for level in levels:
        scratch += level.scratch()
    dma = pltpu.SemaphoreType.DMA
    scratch += [dma((6, 2)), dma((6, 2)), dma((6, ngy)), dma((6, ngy)), dma((2, ngx)), dma((2, ngx))]
    return pl.pallas_call(
        functools.partial(v_cycle_kernel, ngx, ngy, levels),
        out_shape=jax.ShapeDtypeStruct(args[0].shape, f32),
        in_specs=[pl.BlockSpec(memory_space=pltpu.VMEM)] * 5,
        out_specs=pl.BlockSpec(memory_space=pltpu.VMEM),
        scratch_shapes=scratch,
        compiler_params=pltpu.CompilerParams(
            collective_id=0, has_side_effects=True, vmem_limit_bytes=48 * 2**20
        ),
    )(*args)


def solution(mesh):
    ngx, ngy = mesh.shape["gx"], mesh.shape["gy"]
    small = ngy <= 16 and ngx <= 4
    part = functools.partial(fused, ngx, ngy) if small else body
    return jax.shard_map(
        part,
        mesh=mesh,
        in_specs=(P("gy", "gx", None),) * 5,
        out_specs=P("gy", "gx", None),
        check_vma=False,
    )
```

```python
import functools

import jax
import jax.numpy as jnp
from jax import lax
from jax.experimental import pallas as pl
from jax.experimental.pallas import tpu as pltpu
from jax.sharding import PartitionSpec as P

LEVELS = 6


base_shift = 0.001
wall_term = 0.02


def padded(cells, sides, width):
    for axis, dim in sides:
        count = lax.axis_size(axis)
        ends = count - 1
        head = lax.slice_in_dim(cells, 0, width, axis=dim)
        tail = lax.slice_in_dim(cells, cells.shape[dim] - width, cells.shape[dim], axis=dim)
        cells = jnp.concatenate(
            [
                lax.ppermute(tail, axis, [(i, (i + 1) % count) for i in range(ends)]),
                cells,
                lax.ppermute(head, axis, [((i + 1) % count, i) for i in range(ends)]),
            ],
            axis=dim,
        )
    return cells


def swapped(x, axis, stride):
    return lax.ppermute(x, axis, [(i, i ^ 1 << stride) for i in range(lax.axis_size(axis))])


def ahead(field, axis):
    size = field.shape[axis]
    edge = jnp.zeros_like(lax.slice_in_dim(field, 0, 1, axis=axis))
    return jnp.concatenate([lax.slice_in_dim(field, 1, size, axis=axis), edge], axis=axis)


def behind(field, axis):
    size = field.shape[axis]
    edge = jnp.zeros_like(lax.slice_in_dim(field, 0, 1, axis=axis))
    return jnp.concatenate([edge, lax.slice_in_dim(field, 0, size - 1, axis=axis)], axis=axis)


def coarse_sum(field):
    depth, width, height = field.shape
    return field.reshape(depth // 2, 2, width // 2, 2, height // 2, 2).sum(axis=(1, 3, 5))


def coarse_face(face, axis, parity):
    picked = lax.slice_in_dim(face, parity, face.shape[axis], stride=2, axis=axis)
    return 0.125 * coarse_sum(jnp.repeat(picked, 2, axis=axis))


def prolong(field):
    return jnp.repeat(jnp.repeat(jnp.repeat(field, 2, axis=0), 2, axis=1), 2, axis=2)


def upper_flag(bit):
    return lax.axis_index("gy") // 2**bit % 2


def line_factors(lower, diag, upper):
    denoms = [diag[0]]
    ratios = [upper[0] / diag[0]]
    for place in range(1, diag.shape[0]):
        pivot = diag[place] - lower[place] * ratios[place - 1]
        denoms.append(pivot)
        ratios.append(upper[place] / pivot)
    return (denoms, ratios)


def rows_solve(level, rhs):
    lower = level["lower"]
    denoms = level["denoms"]
    ratios = level["ratios"]
    count = rhs.shape[0]
    values = [rhs[0] / denoms[0]]
    for place in range(1, count):
        values.append((rhs[place] - lower[place] * values[place - 1]) / denoms[place])
    result = [values[count - 1]]
    for place in range(count - 2, -1, -1):
        result.append(values[place] - ratios[place] * result[-1])
    return jnp.stack(result[::-1])


def assemble(faces, group):
    face_x, low_x, face_y, low_y, face_z, shift = faces
    low_z = behind(face_z, 2)
    diag = shift + face_x + low_x + face_y + low_y + face_z + low_z
    level = {
        "face_x": face_x,
        "low_x": low_x,
        "face_y": face_y,
        "low_y": low_y,
        "face_z": face_z,
        "low_z": low_z,
        "diag": diag,
        "group": group,
    }
    level["lower"] = -low_y
    denoms, ratios = line_factors(-low_y, diag, -face_y)
    level["denoms"] = denoms
    level["ratios"] = ratios
    blank = jnp.zeros_like(diag)
    level["first_resp"] = rows_solve(level, blank.at[0].set(1.0))
    level["last_resp"] = rows_solve(level, blank.at[-1].set(1.0))
    level["alpha"] = low_y[0] * level["first_resp"][0]
    level["gamma"] = low_y[0] * level["first_resp"][-1]
    level["beta"] = face_y[-1] * level["last_resp"][0]
    level["delta"] = face_y[-1] * level["last_resp"][-1]
    return level


def forward_terms(alpha, beta, gamma, delta, head, tail):
    zeros = jnp.zeros_like(head)
    ones = jnp.ones_like(head)
    return (
        gamma * beta - alpha * delta,
        zeros,
        delta,
        gamma * head - alpha * tail,
        gamma,
        tail,
        -alpha,
        zeros,
        ones,
    )


def chain_forward(earlier, later):
    product = []
    for left_row in range(3):
        for column in range(3):
            product.append(
                later[3 * left_row] * earlier[column]
                + later[3 * left_row + 1] * earlier[3 + column]
                + later[3 * left_row + 2] * earlier[6 + column]
            )
    scale = product[8]
    return tuple((entry / scale for entry in product))


def chain_backward(earlier, later):
    return (later[0] + later[1] * earlier[0], later[1] * earlier[1])


def settle(alpha, beta, head, state):
    carry_q = state[2] / state[8]
    carry_p = state[5] / state[8]
    pivot = 1.0 - alpha * carry_q
    return ((head + alpha * carry_p) / pivot, beta / pivot, carry_q, carry_p)


def reduced_local(alpha, beta, gamma, delta, head, tail):
    zeros = jnp.zeros_like(head[:1])
    ones = jnp.ones_like(head[:1])
    identity = (ones, zeros, zeros, zeros, ones, zeros, zeros, zeros, ones)
    terms = forward_terms(alpha, beta, gamma, delta, head, tail)
    inclusive = lax.associative_scan(chain_forward, terms, axis=0)
    state = tuple(
        (jnp.concatenate([plain, entry[:-1]], axis=0) for plain, entry in zip(identity, inclusive))
    )
    start, slope, carry_q, carry_p = settle(alpha, beta, head, state)
    later = lax.associative_scan(chain_backward, (start, slope), reverse=True, axis=0)
    next_first = jnp.concatenate([later[0][1:], zeros], axis=0)
    first = start + slope * next_first
    return (carry_p + carry_q * first, next_first)


def pick_block(values, index, shape):
    return lax.dynamic_index_in_dim(values, index, 0, keepdims=False).reshape(shape)


def reduced_moved(level, head, tail):
    group = level["group"]
    shape = head.shape
    packed = jnp.stack(
        [level["alpha"], level["beta"], level["gamma"], level["delta"], head, tail]
    ).reshape(6, 1, -1)
    if group == 1:
        moved = lax.all_to_all(packed, "gy", split_axis=2, concat_axis=1, tiled=True)
        prev_last, next_first = reduced_local(
            moved[0], moved[1], moved[2], moved[3], moved[4], moved[5]
        )
        back = lax.all_to_all(
            jnp.stack([prev_last, next_first]), "gy", split_axis=1, concat_axis=2, tiled=True
        )
        return (back[0, 0].reshape(shape), back[1, 0].reshape(shape))
    whole = lax.all_gather(packed, "gy", axis=1, tiled=True)
    whole = whole.reshape(6, whole.shape[1] // group, group, -1)[:, :, 0]
    prev_last, next_first = reduced_local(
        whole[0], whole[1], whole[2], whole[3], whole[4], whole[5]
    )
    index = lax.axis_index("gy") // group
    return (pick_block(prev_last, index, shape), pick_block(next_first, index, shape))


def line_solve(level, rhs):
    local = rows_solve(level, rhs)
    prev_last, next_first = reduced_moved(level, local[0], local[-1])
    return (
        local
        + (level["low_y"][0] * prev_last)[None] * level["first_resp"]
        + (level["face_y"][-1] * next_first)[None] * level["last_resp"]
    )


def neighbour_terms(level, field):
    rim = padded(field, (("gx", 1),), 1)
    return (
        level["face_x"] * rim[:, 2:]
        + level["low_x"] * rim[:, :-2]
        + level["face_z"] * ahead(field, 2)
        + level["low_z"] * behind(field, 2)
    )


def relax(level, field, rhs):
    return line_solve(level, rhs + neighbour_terms(level, field))


def body(source, mask, cond_x, cond_y, cond_z):
    open_cells = (mask != 2).astype(jnp.float32)
    wall = (mask == 1).astype(jnp.float32)
    rim = padded(
        jnp.stack([cond_x * open_cells, cond_y * open_cells, open_cells]), (("gx", 2), ("gy", 1)), 1
    )
    faces = (
        cond_x * open_cells * rim[2, 1:-1, 2:],
        rim[0, 1:-1, :-2] * open_cells,
        cond_y * open_cells * rim[2, 2:, 1:-1],
        rim[1, :-2, 1:-1] * open_cells,
        cond_z * open_cells * ahead(open_cells, 2),
        base_shift + wall_term * wall,
    )
    rhs = source * open_cells
    levels = []
    fields = []
    sources = []
    residual = rhs
    for depth in range(LEVELS):
        group = 1
        if depth > 0:
            face_x, low_x, face_y, low_y, face_z, shift = faces
            faces = (
                coarse_face(face_x, 1, 1),
                coarse_face(low_x, 1, 0),
                coarse_face(face_y, 0, 1),
                coarse_face(low_y, 0, 0),
                coarse_face(face_z, 2, 1),
                0.25 * coarse_sum(shift),
            )
            rhs = 0.25 * coarse_sum(residual)
            if depth >= 2:
                group = 2 ** (depth - 1)
                stacked = jnp.stack((rhs,) + faces)
                partner = swapped(stacked, "gy", depth - 2)
                upper = upper_flag(depth - 2) == 1
                folded = jnp.concatenate(
                    [jnp.where(upper, partner, stacked), jnp.where(upper, stacked, partner)], axis=1
                )
                rhs = folded[0]
                faces = tuple((folded[place] for place in range(1, 7)))
        level = assemble(faces, group)
        field = line_solve(level, rhs)
        if depth == LEVELS - 1:
            field = relax(level, field, rhs)
        else:
            residual = neighbour_terms(level, field)
        levels.append(level)
        fields.append(field)
        sources.append(rhs)
    correction = fields[-1]
    for depth in range(LEVELS - 2, -1, -1):
        if depth + 1 >= 2:
            half = correction.shape[0] // 2
            correction = lax.dynamic_slice_in_dim(correction, upper_flag(depth - 1) * half, half, 0)
        field = fields[depth] + prolong(correction)
        correction = relax(levels[depth], field, sources[depth])
    return correction

MESH = pl.DeviceIdType.MESH
LANES = 128


def looped(count, step, carry, unroll=4):
    while count % unroll:
        unroll //= 2

    def several(outer, carry):
        for inner in range(unroll):
            carry = step(outer * unroll + inner, carry)
        return carry

    return lax.fori_loop(0, count // unroll, several, carry)


def pairing(parity):
    fine = lax.broadcasted_iota(jnp.int32, (LANES, LANES), 0)
    coarse = lax.broadcasted_iota(jnp.int32, (LANES, LANES), 1)
    if parity is None:
        hit = (fine == 2 * coarse) | (fine == 2 * coarse + 1)
    else:
        hit = fine == 2 * coarse + parity
    return jnp.where(hit, 1.0, 0.0).astype(jnp.float32)


def spreading():
    coarse = lax.broadcasted_iota(jnp.int32, (LANES, LANES), 0)
    fine = lax.broadcasted_iota(jnp.int32, (LANES, LANES), 1)
    hit = (fine == 2 * coarse) | (fine == 2 * coarse + 1)
    return jnp.where(hit, 1.0, 0.0).astype(jnp.float32)


def times(left, right):
    right = right.astype(jnp.bfloat16)
    head = left.astype(jnp.bfloat16)
    tail = (left - head.astype(jnp.float32)).astype(jnp.bfloat16)
    return jnp.dot(head, right, preferred_element_type=jnp.float32) + jnp.dot(
        tail, right, preferred_element_type=jnp.float32
    )


def coarsened(field, work, y_odd=False, x_odd=False, z_odd=False, y_summed=False):
    if y_summed:
        summed = field
    else:
        rows, wide, lanes = field.shape
        pairs = field.reshape(rows // 2, 2, wide, lanes)
        summed = pairs[:, 1] if y_odd else pairs[:, 0] + pairs[:, 1]
    rows, wide, lanes = summed.shape
    count = rows * wide
    work[pl.ds(0, count), :] = times(summed.reshape(count, lanes), pairing(1 if z_odd else None))
    result = work[pl.ds(1, count // 2, stride=2), :]
    if not x_odd:
        result = result + work[pl.ds(0, count // 2, stride=2), :]
    return 0.25 * result


def put_rows(target, flat, rows):
    wide = flat.shape[0] // rows
    if wide % 8 == 0:
        target[...] = flat.reshape(rows, wide, LANES)
        return
    target[...] = jnp.zeros_like(target)
    for row in range(rows):
        target[row, pl.ds(0, wide), :] = flat[row * wide : (row + 1) * wide]


def spread_add(target, coarse, wide, work):
    rows = coarse.shape[0]
    half = coarse.shape[1]
    flat = times(coarse.reshape(rows * half, LANES), spreading())
    work[pl.ds(0, rows * half, stride=2), :] = flat
    work[pl.ds(1, rows * half, stride=2), :] = flat
    for row in range(rows):
        extra = work[pl.ds(row * 2 * half, wide), :]
        target[2 * row] = target[2 * row] + extra
        target[2 * row + 1] = target[2 * row + 1] + extra


class Coarse:
    names = ("fx", "lx", "fy", "ly", "fz", "lz", "sh", "rec", "u", "g")

    def __init__(self, rows, width, height):
        self.rows = rows
        self.width = width
        self.height = height
        self.wide = max(8, width)

    def scratch(self):
        return [pltpu.VMEM((self.rows, self.wide, LANES), jnp.float32)] * len(self.names)

    def bind(self, refs):
        for name, ref in zip(self.names, refs):
            setattr(self, name, ref)
        self.halo = None

    def factor(self, edge=None):
        row = lax.broadcasted_iota(jnp.int32, (self.wide, LANES), 0)
        lane = lax.broadcasted_iota(jnp.int32, (self.wide, LANES), 1)
        blank = jnp.where((row >= self.width) | (lane >= self.height), 1.0, 0.0)
        zero = jnp.zeros((self.wide, LANES), jnp.float32)

        def step(y, carry):
            ratio, below = carry
            fx, fy, fz = self.fx[y], self.fy[y], self.fz[y]
            lx = pltpu.roll(fx, 1, 0)
            if edge is not None:
                lx = jnp.where(row == 0, edge(y), lx)
            lz = pltpu.roll(fz, 1, 1)
            diag = self.sh[y] + blank + fx + lx + fy + below + fz + lz
            rec = 1.0 / (diag - below * ratio)
            self.lx[y] = lx
            self.ly[y] = below * rec
            self.lz[y] = lz
            self.rec[y] = rec
            ratio = fy * rec
            self.sh[y] = ratio
            return ratio, fy

        looped(self.rows, step, (zero, zero))

    def beside(self, y):
        u = self.u[y]
        after = pltpu.roll(u, self.wide - 1, 0)
        before = pltpu.roll(u, 1, 0)
        if self.halo is not None:
            row = lax.broadcasted_iota(jnp.int32, (self.wide, LANES), 0)
            before = jnp.where(row == 0, self.halo[0, pl.ds(y, 1), :], before)
            after = jnp.where(row == self.wide - 1, self.halo[1, pl.ds(y, 1), :], after)
        return (
            self.fx[y] * after
            + self.lx[y] * before
            + self.fz[y] * pltpu.roll(u, LANES - 1, 1)
            + self.lz[y] * pltpu.roll(u, 1, 1)
        )

    def solve(self, again):
        zero = jnp.zeros((self.wide, LANES), jnp.float32)

        def down(y, carry):
            right = self.g[y]
            if again:
                right = right + self.beside(y)
            value = right * self.rec[y] + self.ly[y] * carry
            self.u[y] = value
            return value

        def up(step, carry):
            y = self.rows - 1 - step
            value = self.u[y] + self.sh[y] * carry
            self.u[y] = value
            return value

        looped(self.rows, down, zero, 8)
        looped(self.rows, up, zero, 8)

    def residual(self, hold):
        def step(y, carry):
            hold[y] = self.beside(2 * y) + self.beside(2 * y + 1)
            return carry

        looped(self.rows // 2, step, 0)


def v_cycle_kernel(ngx, ngy, levels, *refs):
    given, out = refs[:5], refs[5]
    refs = list(refs[6:])

    def take(count):
        got = refs[:count]
        del refs[:count]
        return got

    rows, wide, lanes = given[0].shape
    gx = lax.axis_index("gx")
    gy = lax.axis_index("gy")
    inside = take(5)
    (source, mask, cond_x, cond_y, cond_z) = inside
    (work, hold) = take(2)
    one = dict(zip(("fx", "lx", "fz", "lz", "rec", "lr", "rat", "first", "last", "f", "u"), take(11)))
    (edge_fy, edge_ly) = take(2)
    (sx, rx, sy, ry) = take(4)
    (coef_s, coef_r, rhs_s, rhs_r) = take(4)
    (face_s, face_r, back_s, back_r, face2_s, face2_r, back2_s, back2_r) = take(8)
    (red, terms, whole_prev, whole_next) = take(4)
    (xu_s, xu_r, xv_s, xv_r, h2_s, h2_r) = take(6)
    (c3_s, c3_r, g3_s, g3_r) = take(4)
    for level in levels:
        level.bind(take(len(Coarse.names)))
    (near_send, near_recv, all_send, all_recv, side_send, side_recv, load_sem) = take(7)
    loads = [pltpu.make_async_copy(a, b, load_sem.at[i]) for i, (a, b) in enumerate(zip(given, inside))]
    for load in loads:
        load.start()
    (tree_send, tree_recv) = take(2)
    peers = [lax.rem(gy + j, ngy) for j in range(1, ngy)]

    def far(src, dst, send, recv, device):
        return pltpu.make_async_remote_copy(
            src_ref=src, dst_ref=dst, send_sem=send, recv_sem=recv, device_id=device, device_id_type=MESH
        )

    def beside_copies(src, dst, slot, axis):
        place, count = (gx, ngx) if axis == 0 else (gy, ngy)
        higher = (gx + 1, gy) if axis == 0 else (gx, gy + 1)
        lower = (gx - 1, gy) if axis == 0 else (gx, gy - 1)
        up = far(src.at[0], dst.at[0], near_send.at[slot, 0], near_recv.at[slot, 0], higher)
        down = far(src.at[1], dst.at[1], near_send.at[slot, 1], near_recv.at[slot, 1], lower)
        return place, count, up, down

    def beside_start(src, dst, slot, axis):
        place, count, up, down = beside_copies(src, dst, slot, axis)

        @pl.when(place < count - 1)
        def _():
            up.start()

        @pl.when(place > 0)
        def _():
            down.start()

    def beside_wait(src, dst, slot, axis):
        place, count, up, down = beside_copies(src, dst, slot, axis)

        @pl.when(place < count - 1)
        def _():
            up.wait_send()
            down.wait_recv()

        @pl.when(place > 0)
        def _():
            down.wait_send()
            up.wait_recv()

    def all_start(src, dst, slot):
        for peer in peers:
            far(src(peer), dst.at[gy], all_send.at[slot], all_recv.at[slot], (gx, peer)).start()

    def all_wait(dst, slot):
        others = dst.at[pl.ds(0, ngy - 1)]
        far(others, others, all_send.at[slot], all_recv.at[slot], (gx, peers[0])).wait()

    far_count = ngy // 4
    place_a = gy // 4
    place_b = lax.rem(gy // 2, 2)
    place_c = lax.rem(gy, 2)

    def tree_slot(k):
        return (lax.rem(k, 2) * 2 + lax.rem(k // 2, 2)) * far_count + k // 4

    def tree_copies(stage):
        if stage == 0:
            copies = []
            for j in range(1, far_count):
                a = lax.rem(place_a + j, far_count)
                slot = tree_slot(gy)
                peer = a * 4 + place_b * 2 + place_c
                there = far_count - j
                copies.append(
                    (
                        far(coef_s, coef_r.at[slot], tree_send.at[j], tree_recv.at[j], (gx, peer)),
                        far(coef_s, coef_r.at[tree_slot(peer)], tree_send.at[j], tree_recv.at[there], (gx, peer)),
                    )
                )
            return copies
        if stage == 1:
            mine = coef_r.at[pl.ds((place_c * 2 + place_b) * far_count, far_count)]
            theirs = coef_r.at[pl.ds((place_c * 2 + 1 - place_b) * far_count, far_count)]
            peer = place_a * 4 + (1 - place_b) * 2 + place_c
        else:
            mine = coef_r.at[pl.ds(place_c * 2 * far_count, 2 * far_count)]
            theirs = coef_r.at[pl.ds((1 - place_c) * 2 * far_count, 2 * far_count)]
            peer = place_a * 4 + place_b * 2 + 1 - place_c
        slot = ngy + stage - 1
        return [
            (
                far(mine, mine, tree_send.at[slot], tree_recv.at[slot], (gx, peer)),
                far(mine, theirs, tree_send.at[slot], tree_recv.at[slot], (gx, peer)),
            )
        ]

    def tree_start(stage):
        for outgoing, incoming in tree_copies(stage):
            outgoing.start()

    def tree_wait(stage):
        for outgoing, incoming in tree_copies(stage):
            outgoing.wait_send()
            incoming.wait_recv()

    def side_start(src, dst, slot):
        for j in range(1, ngx):
            peer = lax.rem(gx + j, ngx)
            far(src, dst.at[gx], side_send.at[slot, j], side_recv.at[slot, gx], (peer, gy)).start()

    def side_wait(src, dst, slot):
        for j in range(1, ngx):
            peer = lax.rem(gx + j, ngx)
            far(src, dst.at[peer], side_send.at[slot, j], side_recv.at[slot, peer], (peer, gy)).wait()

    for ref in (rx, ry, xu_r, xv_r, h2_r):
        ref[...] = jnp.zeros_like(ref)
    barrier = pltpu.get_barrier_semaphore()

    for peer in peers:
        pl.semaphore_signal(barrier, inc=1, device_id=(gx, peer), device_id_type=MESH)
    for j in range(1, ngx):
        pl.semaphore_signal(barrier, inc=1, device_id=(lax.rem(gx + j, ngx), gy), device_id_type=MESH)
    for load in loads:
        load.wait()
    pl.semaphore_wait(barrier, ngy - 1 + ngx - 1)

    row = lax.broadcasted_iota(jnp.int32, (wide, lanes), 0)
    lane = lax.broadcasted_iota(jnp.int32, (wide, lanes), 1)
    opened = [jnp.where(mask[y] != 2, 1.0, 0.0) for y in range(rows)]
    for y in range(rows):
        sx[0, pl.ds(y, 1), :] = (cond_x[y] * opened[y])[wide - 1 :]
        sx[1, pl.ds(y, 1), :] = opened[y][:1]
    sy[0] = cond_y[rows - 1] * opened[rows - 1]
    sy[1] = opened[0]
    beside_start(sx, rx, 0, 0)
    beside_start(sy, ry, 1, 1)
    beside_wait(sx, rx, 0, 0)
    beside_wait(sy, ry, 1, 1)
    faces_y = []
    lows_y = [ry[0] * opened[0]]
    shifts = []
    for y in range(rows):
        now = opened[y]
        cx = cond_x[y] * now
        one["fx"][y] = cx * jnp.where(row == wide - 1, rx[1, pl.ds(y, 1), :], pltpu.roll(now, wide - 1, 0))
        one["lx"][y] = now * jnp.where(row == 0, rx[0, pl.ds(y, 1), :], pltpu.roll(cx, 1, 0))
        above = opened[y + 1] if y + 1 < rows else ry[1]
        faces_y.append(cond_y[y] * now * above)
        if y + 1 < rows:
            lows_y.append(faces_y[y])
        fz = cond_z[y] * now * jnp.where(lane == lanes - 1, 0.0, pltpu.roll(now, lanes - 1, 1))
        one["fz"][y] = fz
        one["lz"][y] = pltpu.roll(fz, 1, 1)
        shifts.append(base_shift + wall_term * jnp.where(mask[y] == 1, 1.0, 0.0))
        one["f"][y] = source[y] * now
    edge_fy[...] = faces_y[rows - 1]
    edge_ly[...] = lows_y[0]

    recs = []
    ratio = None
    for y in range(rows):
        diag = shifts[y] + one["fx"][y] + one["lx"][y] + faces_y[y] + lows_y[y] + one["fz"][y] + one["lz"][y]
        if y:
            diag = diag - lows_y[y] * ratio
        rec = 1.0 / diag
        ratio = faces_y[y] * rec
        recs.append(rec)
        one["rec"][y] = rec
        one["rat"][y] = ratio
        one["lr"][y] = lows_y[y] * rec

    def block_solve(right):
        value = right[0] * one["rec"][0]
        values = [value]
        for y in range(1, rows):
            value = right[y] * one["rec"][y] + one["lr"][y] * value
            values.append(value)
        for y in range(rows - 2, -1, -1):
            values[y] = values[y] + one["rat"][y] * values[y + 1]
        return values

    firsts = [recs[0]]
    for y in range(1, rows):
        firsts.append(one["lr"][y] * firsts[-1])
    lasts = [None] * (rows - 1) + [recs[rows - 1]]
    for y in range(rows - 2, -1, -1):
        firsts[y] = firsts[y] + one["rat"][y] * firsts[y + 1]
        lasts[y] = one["rat"][y] * lasts[y + 1]
    low, high = edge_ly[...], edge_fy[...]
    for y in range(rows):
        firsts[y] = low * firsts[y]
        lasts[y] = high * lasts[y]
        one["first"][y] = firsts[y]
        one["last"][y] = lasts[y]
    share = wide // ngy

    def shared(target, values):
        for place, value in enumerate(values):
            for owner in range(ngy):
                target[owner, place] = value[owner * share : (owner + 1) * share]

    def reduced(rhs, send):
        zero = jnp.zeros((share, lanes), jnp.float32)

        def down(k, carry):
            p = carry
            start = (rhs[k, 0] + face_r[k, 0] * p) * red[k, 1]
            terms[k, 0] = start
            terms[k, 1] = p
            return rhs[k, 1] + face_r[k, 2] * (p + red[k, 0] * start)

        def up(step, after):
            k = ngy - 1 - step
            first = terms[k, 0] + red[k, 2] * after
            send[k, 0] = terms[k, 1] + red[k, 0] * first
            send[k, 1] = after
            return first

        looped(ngy, down, zero)
        looped(ngy, up, zero)

    def reduced_factor():
        def step(k, q):
            inv = 1.0 / (1.0 - face_r[k, 0] * q)
            slope = face_r[k, 1] * inv
            red[k, 0] = q
            red[k, 1] = inv
            red[k, 2] = slope
            return face_r[k, 3] + face_r[k, 2] * q * slope

        looped(ngy, step, jnp.zeros((share, lanes), jnp.float32))

    def joined(local, got):
        for owner in range(ngy):
            whole_prev[pl.ds(owner * share, share), :] = got[owner, 0]
            whole_next[pl.ds(owner * share, share), :] = got[owner, 1]
        prev, after = whole_prev[...], whole_next[...]
        return [local[y] + prev * one["first"][y] + after * one["last"][y] for y in range(rows)]

    local = block_solve([one["f"][y] for y in range(rows)])
    shared(face_s, [firsts[0], lasts[0], firsts[rows - 1], lasts[rows - 1], local[0], local[rows - 1]])
    face_r[gy] = face_s[gy]
    all_start(lambda peer: face_s.at[peer], face_r, 1)

    half = rows // 2
    quarter = rows // 4
    wide2 = wide // 2
    both = lanes // 2

    def packed(flat):
        whole = flat.reshape(half, wide2, lanes)
        return whole[:quarter] + pltpu.roll(whole[quarter:], both, 2)

    coarse_fx = coarsened(one["fx"][...], work, x_odd=True)
    coef_s[pl.ds(0, quarter)] = packed(coarse_fx)
    coef_s[pl.ds(quarter, quarter)] = packed(coarsened(jnp.stack(faces_y), work, y_odd=True))
    coef_s[pl.ds(2 * quarter, quarter)] = packed(coarsened(one["fz"][...], work, z_odd=True))
    coef_s[pl.ds(3 * quarter, quarter)] = packed(coarsened(jnp.stack(shifts), work))
    lx_all = one["lx"][...].reshape(half, 2, wide, lanes)
    lx_rows = (lx_all[:, 0] + lx_all[:, 1]).reshape(half * wide, lanes)
    work[pl.ds(0, half * wide), :] = times(lx_rows, pairing(None))
    for y in range(half):
        coef_s[4 * quarter, pl.ds(y, 1), :] = 0.25 * work[pl.ds(y * wide, 1), :]
    coef_r[tree_slot(gy)] = coef_s[...]
    tree_start(0)
    all_wait(face_r, 1)
    reduced_factor()
    reduced(face_r.at[:, pl.ds(4, 2)], back_s)
    back_r[gy] = back_s[gy]
    all_start(lambda peer: back_s.at[peer], back_r, 2)
    tree_wait(0)
    tree_start(1)
    all_wait(back_r, 2)
    values = joined(local, back_r)

    def outer_planes(values, target):
        for y in range(rows):
            target[0, pl.ds(y, 1), :] = values[y][wide - 1 :]
            target[1, pl.ds(y, 1), :] = values[y][:1]

    def beside_one(y, u, got):
        return (
            one["fx"][y] * jnp.where(row == wide - 1, got[1, pl.ds(y, 1), :], pltpu.roll(u, wide - 1, 0))
            + one["lx"][y] * jnp.where(row == 0, got[0, pl.ds(y, 1), :], pltpu.roll(u, 1, 0))
            + one["fz"][y] * pltpu.roll(u, lanes - 1, 1)
            + one["lz"][y] * pltpu.roll(u, 1, 1)
        )

    outer_planes(values, xu_s)
    beside_start(xu_s, xu_r, 2, 0)
    for y in range(rows):
        one["u"][y] = values[y]
    tree_wait(1)
    tree_start(2)
    beside_wait(xu_s, xu_r, 2, 0)
    left = jnp.stack([beside_one(y, values[y], xu_r) for y in range(rows)])
    rhs_s[...] = packed(coarsened(left, work))
    rhs_r[gy] = rhs_s[...]
    all_start(lambda peer: rhs_s, rhs_r, 3)

    two, three = levels[0], levels[1]
    used = lax.broadcasted_iota(jnp.int32, (wide2, lanes), 1) < both

    def unpack2(target, block, k):
        for y in range(quarter):
            pair = block(y)
            target[half * k + y] = jnp.where(used, pair, 0.0)
            target[half * k + quarter + y] = jnp.where(used, pltpu.roll(pair, both, 1), 0.0)

    tree_wait(2)

    def take_coefs(k, carry):
        for place, target in enumerate((two.fx, two.fy, two.fz, two.sh)):
            unpack2(target, lambda y: coef_r[tree_slot(k), place * quarter + y], k)
        return carry

    lax.fori_loop(0, ngy, take_coefs, 0)

    rows3 = three.rows
    part3 = rows3 // 4
    wide3 = wide2 // 2
    step3 = lanes // 4

    def packed3(flat):
        whole = flat.reshape(rows3, wide3, lanes)
        total = whole[:part3]
        for j in range(1, 4):
            total = total + pltpu.roll(whole[j * part3 : (j + 1) * part3], j * step3, 2)
        return total

    used3 = lax.broadcasted_iota(jnp.int32, (part3, wide3, lanes), 2) < step3

    def unpack3(target, got):
        for g in range(ngx):
            block = got(g)
            for j in range(4):
                turned = block if j == 0 else pltpu.roll(block, lanes - j * step3, 2)
                target[pl.ds(j * part3, part3), pl.ds(g * wide3, wide3), :] = jnp.where(used3, turned, 0.0)

    c3_s[0] = packed3(coarsened(two.fx[...], work, x_odd=True))
    c3_s[1] = packed3(coarsened(two.fy[...], work, y_odd=True))
    c3_s[2] = packed3(coarsened(two.fz[...], work, z_odd=True))
    c3_s[3] = packed3(coarsened(two.sh[...], work))
    c3_r[gx] = c3_s[...]
    side_start(c3_s, c3_r, 0)

    def edge2(y):
        return h2_s[0, pl.ds(y, 1), :]

    def take_edges(k, carry):
        for y in range(half):
            h2_s[0, pl.ds(half * k + y, 1), :] = coef_r[tree_slot(k), 4 * quarter, pl.ds(y, 1), :]
        return carry

    lax.fori_loop(0, ngy, take_edges, 0)
    two.factor(edge2)
    all_wait(rhs_r, 3)

    def take_rhs(k, carry):
        unpack2(two.g, lambda y: rhs_r[k, y], k)
        return carry

    lax.fori_loop(0, ngy, take_rhs, 0)
    two.solve(False)

    def outer_two(target):
        def step(y, carry):
            target[0, pl.ds(y, 1), :] = two.u[y, pl.ds(wide2 - 1, 1), :]
            target[1, pl.ds(y, 1), :] = two.u[y, pl.ds(0, 1), :]
            return carry

        looped(two.rows, step, 0)

    outer_two(h2_s)
    beside_start(h2_s, h2_r, 3, 0)
    side_wait(c3_s, c3_r, 0)
    for place, target in enumerate((three.fx, three.fy, three.fz, three.sh)):
        unpack3(target, lambda g: c3_r[g, place])
    for fine, level in zip(levels[1:], levels[2:]):
        put_rows(level.fx, coarsened(fine.fx[...], work, x_odd=True), level.rows)
        put_rows(level.fy, coarsened(fine.fy[...], work, y_odd=True), level.rows)
        put_rows(level.fz, coarsened(fine.fz[...], work, z_odd=True), level.rows)
        put_rows(level.sh, coarsened(fine.sh[...], work), level.rows)
    for level in levels[1:]:
        level.factor()
    beside_wait(h2_s, h2_r, 3, 0)
    two.halo = h2_r
    two.residual(hold)
    g3_s[...] = packed3(coarsened(hold[...], work, y_summed=True))
    g3_r[gx] = g3_s[...]
    side_start(g3_s, g3_r, 1)
    side_wait(g3_s, g3_r, 1)
    unpack3(three.g, lambda g: g3_r[g])
    for fine, level in zip(levels[1:], levels[2:]):
        fine.solve(False)
        part = hold.at[pl.ds(0, fine.rows // 2), pl.ds(0, fine.wide)]
        fine.residual(part)
        put_rows(level.g, coarsened(part[...], work, y_summed=True), level.rows)
    levels[-1].solve(False)
    levels[-1].solve(True)
    for fine, level in zip(levels[-2:0:-1], levels[:1:-1]):
        spread_add(fine.u, level.u[...], fine.wide, work)
        fine.solve(True)
    spread_add(two.u, three.u[:, pl.ds(pl.multiple_of(gx * wide3, 8), wide3), :], wide2, work)
    for side, plane in enumerate((lax.max(gx * wide3 - 1, 0), lax.min((gx + 1) * wide3, three.width - 1))):

        def pick(y, carry):
            work[pl.ds(y, 1), :] = three.u[y, pl.ds(plane, 1), :]
            return carry

        looped(rows3, pick, 0)
        extra = times(work[pl.ds(0, rows3), :], spreading())
        work[pl.ds(0, rows3, stride=2), :] = extra
        work[pl.ds(1, rows3, stride=2), :] = extra
        h2_r[side] = h2_r[side] + work[pl.ds(0, 2 * rows3), :]
    two.solve(True)
    spread_add(one["u"], two.u[pl.ds(gy * half, half)], wide, work)
    values = [one["u"][y] for y in range(rows)]
    outer_planes(values, xv_s)
    beside_start(xv_s, xv_r, 5, 0)
    beside_wait(xv_s, xv_r, 5, 0)
    local = block_solve([one["f"][y] + beside_one(y, values[y], xv_r) for y in range(rows)])
    shared(face2_s, [local[0], local[rows - 1]])
    face2_r[gy] = face2_s[gy]
    all_start(lambda peer: face2_s.at[peer], face2_r, 4)
    all_wait(face2_r, 4)
    reduced(face2_r, back2_s)
    back2_r[gy] = back2_s[gy]
    all_start(lambda peer: back2_s.at[peer], back2_r, 5)
    all_wait(back2_r, 5)
    values = joined(local, back2_r)
    for y in range(rows):
        out[y] = values[y]


def fused(ngx, ngy, *args):
    rows, wide, lanes = args[0].shape
    f32 = jnp.float32
    levels = [Coarse(rows // 2 * ngy, wide // 2, lanes // 2)]
    for depth in range(2, LEVELS):
        whole = wide * ngx >> depth
        levels.append(Coarse(rows * ngy >> depth, whole, lanes >> depth))
    two, three = levels[:2]
    share = wide // ngy
    quarter = rows // 4
    wide2 = wide // 2

    def room(*shape):
        return pltpu.VMEM(shape, f32)

    part3 = three.rows // 4
    wide3 = wide2 // 2
    most = max(rows * wide, two.rows * two.wide, three.rows * three.wide)
    scratch = [pltpu.VMEM(arg.shape, arg.dtype) for arg in args]
    scratch += [room(most, lanes), room(two.rows // 2, two.wide, lanes)]
    scratch += [room(rows, wide, lanes)] * 11
    scratch += [room(wide, lanes)] * 2
    scratch += [room(2, rows, lanes)] * 2 + [room(2, wide, lanes)] * 2
    count = 4 * quarter + 1
    scratch += [room(count, wide2, lanes), room(ngy, count, wide2, lanes)]
    scratch += [room(quarter, wide2, lanes), room(ngy, quarter, wide2, lanes)]
    scratch += [room(ngy, 6, share, lanes)] * 2 + [room(ngy, 2, share, lanes)] * 6
    scratch += [room(ngy, 3, share, lanes), room(ngy, 2, share, lanes)]
    scratch += [room(wide, lanes)] * 2
    scratch += [room(2, rows, lanes)] * 4 + [room(2, two.rows, lanes)] * 2
    scratch += [room(4, part3, wide3, lanes), room(ngx, 4, part3, wide3, lanes)]
    scratch += [room(part3, wide3, lanes), room(ngx, part3, wide3, lanes)]
    for level in levels:
        scratch += level.scratch()
    dma = pltpu.SemaphoreType.DMA
    scratch += [dma((6, 2)), dma((6, 2)), dma((6,)), dma((6,)), dma((2, ngx)), dma((2, ngx)), dma((5,))]
    scratch += [dma((ngy + 2,)), dma((ngy + 2,))]
    return pl.pallas_call(
        functools.partial(v_cycle_kernel, ngx, ngy, levels),
        out_shape=jax.ShapeDtypeStruct(args[0].shape, f32),
        in_specs=[pl.BlockSpec(memory_space=pltpu.HBM)] * 5,
        out_specs=pl.BlockSpec(memory_space=pltpu.VMEM),
        scratch_shapes=scratch,
        compiler_params=pltpu.CompilerParams(
            collective_id=0, has_side_effects=True, vmem_limit_bytes=63 * 2**20
        ),
    )(*args)


def solution(mesh):
    ngx, ngy = mesh.shape["gx"], mesh.shape["gy"]
    small = ngy == 16 and ngx <= 4
    part = functools.partial(fused, ngx, ngy) if small else body
    return jax.shard_map(
        part,
        mesh=mesh,
        in_specs=(P("gy", "gx", None),) * 5,
        out_specs=P("gy", "gx", None),
        check_vma=False,
    )
```

```python
import functools

import jax
import jax.numpy as jnp
from jax import lax
from jax.experimental import pallas as pl
from jax.experimental.pallas import tpu as pltpu
from jax.sharding import PartitionSpec as P

LEVELS = 6


base_shift = 0.001
wall_term = 0.02


def padded(cells, sides, width):
    for axis, dim in sides:
        count = lax.axis_size(axis)
        ends = count - 1
        head = lax.slice_in_dim(cells, 0, width, axis=dim)
        tail = lax.slice_in_dim(cells, cells.shape[dim] - width, cells.shape[dim], axis=dim)
        cells = jnp.concatenate(
            [
                lax.ppermute(tail, axis, [(i, (i + 1) % count) for i in range(ends)]),
                cells,
                lax.ppermute(head, axis, [((i + 1) % count, i) for i in range(ends)]),
            ],
            axis=dim,
        )
    return cells


def swapped(x, axis, stride):
    return lax.ppermute(x, axis, [(i, i ^ 1 << stride) for i in range(lax.axis_size(axis))])


def ahead(field, axis):
    size = field.shape[axis]
    edge = jnp.zeros_like(lax.slice_in_dim(field, 0, 1, axis=axis))
    return jnp.concatenate([lax.slice_in_dim(field, 1, size, axis=axis), edge], axis=axis)


def behind(field, axis):
    size = field.shape[axis]
    edge = jnp.zeros_like(lax.slice_in_dim(field, 0, 1, axis=axis))
    return jnp.concatenate([edge, lax.slice_in_dim(field, 0, size - 1, axis=axis)], axis=axis)


def coarse_sum(field):
    depth, width, height = field.shape
    return field.reshape(depth // 2, 2, width // 2, 2, height // 2, 2).sum(axis=(1, 3, 5))


def coarse_face(face, axis, parity):
    picked = lax.slice_in_dim(face, parity, face.shape[axis], stride=2, axis=axis)
    return 0.125 * coarse_sum(jnp.repeat(picked, 2, axis=axis))


def prolong(field):
    return jnp.repeat(jnp.repeat(jnp.repeat(field, 2, axis=0), 2, axis=1), 2, axis=2)


def upper_flag(bit):
    return lax.axis_index("gy") // 2**bit % 2


def line_factors(lower, diag, upper):
    denoms = [diag[0]]
    ratios = [upper[0] / diag[0]]
    for place in range(1, diag.shape[0]):
        pivot = diag[place] - lower[place] * ratios[place - 1]
        denoms.append(pivot)
        ratios.append(upper[place] / pivot)
    return (denoms, ratios)


def rows_solve(level, rhs):
    lower = level["lower"]
    denoms = level["denoms"]
    ratios = level["ratios"]
    count = rhs.shape[0]
    values = [rhs[0] / denoms[0]]
    for place in range(1, count):
        values.append((rhs[place] - lower[place] * values[place - 1]) / denoms[place])
    result = [values[count - 1]]
    for place in range(count - 2, -1, -1):
        result.append(values[place] - ratios[place] * result[-1])
    return jnp.stack(result[::-1])


def assemble(faces, group):
    face_x, low_x, face_y, low_y, face_z, shift = faces
    low_z = behind(face_z, 2)
    diag = shift + face_x + low_x + face_y + low_y + face_z + low_z
    level = {
        "face_x": face_x,
        "low_x": low_x,
        "face_y": face_y,
        "low_y": low_y,
        "face_z": face_z,
        "low_z": low_z,
        "diag": diag,
        "group": group,
    }
    level["lower"] = -low_y
    denoms, ratios = line_factors(-low_y, diag, -face_y)
    level["denoms"] = denoms
    level["ratios"] = ratios
    blank = jnp.zeros_like(diag)
    level["first_resp"] = rows_solve(level, blank.at[0].set(1.0))
    level["last_resp"] = rows_solve(level, blank.at[-1].set(1.0))
    level["alpha"] = low_y[0] * level["first_resp"][0]
    level["gamma"] = low_y[0] * level["first_resp"][-1]
    level["beta"] = face_y[-1] * level["last_resp"][0]
    level["delta"] = face_y[-1] * level["last_resp"][-1]
    return level


def forward_terms(alpha, beta, gamma, delta, head, tail):
    zeros = jnp.zeros_like(head)
    ones = jnp.ones_like(head)
    return (
        gamma * beta - alpha * delta,
        zeros,
        delta,
        gamma * head - alpha * tail,
        gamma,
        tail,
        -alpha,
        zeros,
        ones,
    )


def chain_forward(earlier, later):
    product = []
    for left_row in range(3):
        for column in range(3):
            product.append(
                later[3 * left_row] * earlier[column]
                + later[3 * left_row + 1] * earlier[3 + column]
                + later[3 * left_row + 2] * earlier[6 + column]
            )
    scale = product[8]
    return tuple((entry / scale for entry in product))


def chain_backward(earlier, later):
    return (later[0] + later[1] * earlier[0], later[1] * earlier[1])


def settle(alpha, beta, head, state):
    carry_q = state[2] / state[8]
    carry_p = state[5] / state[8]
    pivot = 1.0 - alpha * carry_q
    return ((head + alpha * carry_p) / pivot, beta / pivot, carry_q, carry_p)


def reduced_local(alpha, beta, gamma, delta, head, tail):
    zeros = jnp.zeros_like(head[:1])
    ones = jnp.ones_like(head[:1])
    identity = (ones, zeros, zeros, zeros, ones, zeros, zeros, zeros, ones)
    terms = forward_terms(alpha, beta, gamma, delta, head, tail)
    inclusive = lax.associative_scan(chain_forward, terms, axis=0)
    state = tuple(
        (jnp.concatenate([plain, entry[:-1]], axis=0) for plain, entry in zip(identity, inclusive))
    )
    start, slope, carry_q, carry_p = settle(alpha, beta, head, state)
    later = lax.associative_scan(chain_backward, (start, slope), reverse=True, axis=0)
    next_first = jnp.concatenate([later[0][1:], zeros], axis=0)
    first = start + slope * next_first
    return (carry_p + carry_q * first, next_first)


def pick_block(values, index, shape):
    return lax.dynamic_index_in_dim(values, index, 0, keepdims=False).reshape(shape)


def reduced_moved(level, head, tail):
    group = level["group"]
    shape = head.shape
    packed = jnp.stack(
        [level["alpha"], level["beta"], level["gamma"], level["delta"], head, tail]
    ).reshape(6, 1, -1)
    if group == 1:
        moved = lax.all_to_all(packed, "gy", split_axis=2, concat_axis=1, tiled=True)
        prev_last, next_first = reduced_local(
            moved[0], moved[1], moved[2], moved[3], moved[4], moved[5]
        )
        back = lax.all_to_all(
            jnp.stack([prev_last, next_first]), "gy", split_axis=1, concat_axis=2, tiled=True
        )
        return (back[0, 0].reshape(shape), back[1, 0].reshape(shape))
    whole = lax.all_gather(packed, "gy", axis=1, tiled=True)
    whole = whole.reshape(6, whole.shape[1] // group, group, -1)[:, :, 0]
    prev_last, next_first = reduced_local(
        whole[0], whole[1], whole[2], whole[3], whole[4], whole[5]
    )
    index = lax.axis_index("gy") // group
    return (pick_block(prev_last, index, shape), pick_block(next_first, index, shape))


def line_solve(level, rhs):
    local = rows_solve(level, rhs)
    prev_last, next_first = reduced_moved(level, local[0], local[-1])
    return (
        local
        + (level["low_y"][0] * prev_last)[None] * level["first_resp"]
        + (level["face_y"][-1] * next_first)[None] * level["last_resp"]
    )


def neighbour_terms(level, field):
    rim = padded(field, (("gx", 1),), 1)
    return (
        level["face_x"] * rim[:, 2:]
        + level["low_x"] * rim[:, :-2]
        + level["face_z"] * ahead(field, 2)
        + level["low_z"] * behind(field, 2)
    )


def relax(level, field, rhs):
    return line_solve(level, rhs + neighbour_terms(level, field))


def body(source, mask, cond_x, cond_y, cond_z):
    open_cells = (mask != 2).astype(jnp.float32)
    wall = (mask == 1).astype(jnp.float32)
    rim = padded(
        jnp.stack([cond_x * open_cells, cond_y * open_cells, open_cells]), (("gx", 2), ("gy", 1)), 1
    )
    faces = (
        cond_x * open_cells * rim[2, 1:-1, 2:],
        rim[0, 1:-1, :-2] * open_cells,
        cond_y * open_cells * rim[2, 2:, 1:-1],
        rim[1, :-2, 1:-1] * open_cells,
        cond_z * open_cells * ahead(open_cells, 2),
        base_shift + wall_term * wall,
    )
    rhs = source * open_cells
    levels = []
    fields = []
    sources = []
    residual = rhs
    for depth in range(LEVELS):
        group = 1
        if depth > 0:
            face_x, low_x, face_y, low_y, face_z, shift = faces
            faces = (
                coarse_face(face_x, 1, 1),
                coarse_face(low_x, 1, 0),
                coarse_face(face_y, 0, 1),
                coarse_face(low_y, 0, 0),
                coarse_face(face_z, 2, 1),
                0.25 * coarse_sum(shift),
            )
            rhs = 0.25 * coarse_sum(residual)
            if depth >= 2:
                group = 2 ** (depth - 1)
                stacked = jnp.stack((rhs,) + faces)
                partner = swapped(stacked, "gy", depth - 2)
                upper = upper_flag(depth - 2) == 1
                folded = jnp.concatenate(
                    [jnp.where(upper, partner, stacked), jnp.where(upper, stacked, partner)], axis=1
                )
                rhs = folded[0]
                faces = tuple((folded[place] for place in range(1, 7)))
        level = assemble(faces, group)
        field = line_solve(level, rhs)
        if depth == LEVELS - 1:
            field = relax(level, field, rhs)
        else:
            residual = neighbour_terms(level, field)
        levels.append(level)
        fields.append(field)
        sources.append(rhs)
    correction = fields[-1]
    for depth in range(LEVELS - 2, -1, -1):
        if depth + 1 >= 2:
            half = correction.shape[0] // 2
            correction = lax.dynamic_slice_in_dim(correction, upper_flag(depth - 1) * half, half, 0)
        field = fields[depth] + prolong(correction)
        correction = relax(levels[depth], field, sources[depth])
    return correction

MESH = pl.DeviceIdType.MESH
LANES = 128


def looped(count, step, carry, unroll=4):
    while count % unroll:
        unroll //= 2

    def several(outer, carry):
        for inner in range(unroll):
            carry = step(outer * unroll + inner, carry)
        return carry

    return lax.fori_loop(0, count // unroll, several, carry)


def pairing(parity):
    fine = lax.broadcasted_iota(jnp.int32, (LANES, LANES), 0)
    coarse = lax.broadcasted_iota(jnp.int32, (LANES, LANES), 1)
    if parity is None:
        hit = (fine == 2 * coarse) | (fine == 2 * coarse + 1)
    else:
        hit = fine == 2 * coarse + parity
    return jnp.where(hit, 1.0, 0.0).astype(jnp.float32)


def spreading():
    coarse = lax.broadcasted_iota(jnp.int32, (LANES, LANES), 0)
    fine = lax.broadcasted_iota(jnp.int32, (LANES, LANES), 1)
    hit = (fine == 2 * coarse) | (fine == 2 * coarse + 1)
    return jnp.where(hit, 1.0, 0.0).astype(jnp.float32)


def times(left, right):
    right = right.astype(jnp.bfloat16)
    head = left.astype(jnp.bfloat16)
    tail = (left - head.astype(jnp.float32)).astype(jnp.bfloat16)
    return jnp.dot(head, right, preferred_element_type=jnp.float32) + jnp.dot(
        tail, right, preferred_element_type=jnp.float32
    )


def coarsened(field, work, y_odd=False, x_odd=False, z_odd=False, y_summed=False):
    if y_summed:
        summed = field
    else:
        rows, wide, lanes = field.shape
        pairs = field.reshape(rows // 2, 2, wide, lanes)
        summed = pairs[:, 1] if y_odd else pairs[:, 0] + pairs[:, 1]
    rows, wide, lanes = summed.shape
    count = rows * wide
    work[pl.ds(0, count), :] = times(summed.reshape(count, lanes), pairing(1 if z_odd else None))
    result = work[pl.ds(1, count // 2, stride=2), :]
    if not x_odd:
        result = result + work[pl.ds(0, count // 2, stride=2), :]
    return 0.25 * result


def put_rows(target, flat, rows):
    wide = flat.shape[0] // rows
    if wide % 8 == 0:
        target[...] = flat.reshape(rows, wide, LANES)
        return
    target[...] = jnp.zeros_like(target)
    for row in range(rows):
        target[row, pl.ds(0, wide), :] = flat[row * wide : (row + 1) * wide]


def spread_add(target, coarse, wide, work):
    rows = coarse.shape[0]
    half = coarse.shape[1]
    flat = times(coarse.reshape(rows * half, LANES), spreading())
    work[pl.ds(0, rows * half, stride=2), :] = flat
    work[pl.ds(1, rows * half, stride=2), :] = flat
    for row in range(rows):
        extra = work[pl.ds(row * 2 * half, wide), :]
        target[2 * row] = target[2 * row] + extra
        target[2 * row + 1] = target[2 * row + 1] + extra


class Coarse:
    names = ("fx", "lx", "fy", "ly", "fz", "lz", "sh", "rec", "u", "g")

    def __init__(self, rows, width, height):
        self.rows = rows
        self.width = width
        self.height = height
        self.wide = max(8, width)

    def scratch(self):
        return [pltpu.VMEM((self.rows, self.wide, LANES), jnp.float32)] * len(self.names)

    def bind(self, refs):
        for name, ref in zip(self.names, refs):
            setattr(self, name, ref)
        self.halo = None

    def factor(self, edge=None):
        row = lax.broadcasted_iota(jnp.int32, (self.wide, LANES), 0)
        lane = lax.broadcasted_iota(jnp.int32, (self.wide, LANES), 1)
        blank = jnp.where((row >= self.width) | (lane >= self.height), 1.0, 0.0)
        zero = jnp.zeros((self.wide, LANES), jnp.float32)

        def step(y, carry):
            ratio, below = carry
            fx, fy, fz = self.fx[y], self.fy[y], self.fz[y]
            lx = pltpu.roll(fx, 1, 0)
            if edge is not None:
                lx = jnp.where(row == 0, edge(y), lx)
            lz = pltpu.roll(fz, 1, 1)
            diag = self.sh[y] + blank + fx + lx + fy + below + fz + lz
            rec = 1.0 / (diag - below * ratio)
            self.lx[y] = lx
            self.ly[y] = below * rec
            self.lz[y] = lz
            self.rec[y] = rec
            ratio = fy * rec
            self.sh[y] = ratio
            return ratio, fy

        looped(self.rows, step, (zero, zero))

    def beside(self, y):
        u = self.u[y]
        after = pltpu.roll(u, self.wide - 1, 0)
        before = pltpu.roll(u, 1, 0)
        if self.halo is not None:
            row = lax.broadcasted_iota(jnp.int32, (self.wide, LANES), 0)
            before = jnp.where(row == 0, self.halo[0, pl.ds(y, 1), :], before)
            after = jnp.where(row == self.wide - 1, self.halo[1, pl.ds(y, 1), :], after)
        return (
            self.fx[y] * after
            + self.lx[y] * before
            + self.fz[y] * pltpu.roll(u, LANES - 1, 1)
            + self.lz[y] * pltpu.roll(u, 1, 1)
        )

    def solve(self, again):
        zero = jnp.zeros((self.wide, LANES), jnp.float32)

        def down(y, carry):
            right = self.g[y]
            if again:
                right = right + self.beside(y)
            value = right * self.rec[y] + self.ly[y] * carry
            self.u[y] = value
            return value

        def up(step, carry):
            y = self.rows - 1 - step
            value = self.u[y] + self.sh[y] * carry
            self.u[y] = value
            return value

        looped(self.rows, down, zero, 16)
        looped(self.rows, up, zero, 16)

    def residual(self, hold):
        def step(y, carry):
            hold[y] = self.beside(2 * y) + self.beside(2 * y + 1)
            return carry

        looped(self.rows // 2, step, 0, 8)


def v_cycle_kernel(ngx, ngy, levels, *refs):
    given, out = refs[:5], refs[5]
    refs = list(refs[6:])

    def take(count):
        got = refs[:count]
        del refs[:count]
        return got

    rows, wide, lanes = given[0].shape
    gx = lax.axis_index("gx")
    gy = lax.axis_index("gy")
    inside = take(5)
    (source, mask, cond_x, cond_y, cond_z) = inside
    (work, hold) = take(2)
    one = dict(zip(("fx", "lx", "fz", "lz", "rec", "lr", "rat", "first", "last", "f", "u"), take(11)))
    (edge_fy, edge_ly) = take(2)
    (sx, rx, sy, ry) = take(4)
    (coef_s, coef_r, rhs_s, rhs_r) = take(4)
    (face_s, face_r, back_s, back_r, face2_s, face2_r, back2_s, back2_r) = take(8)
    (red, terms, whole_prev, whole_next) = take(4)
    (xu_s, xu_r, xv_s, xv_r, h2_s, h2_r) = take(6)
    (c3_s, c3_r, g3_s, g3_r) = take(4)
    for level in levels:
        level.bind(take(len(Coarse.names)))
    (near_send, near_recv, all_send, all_recv, side_send, side_recv, load_sem) = take(7)
    loads = [pltpu.make_async_copy(a, b, load_sem.at[i]) for i, (a, b) in enumerate(zip(given, inside))]
    for load in loads:
        load.start()
    (tree_send, tree_recv) = take(2)
    peers = [lax.rem(gy + j, ngy) for j in range(1, ngy)]

    def far(src, dst, send, recv, device):
        return pltpu.make_async_remote_copy(
            src_ref=src, dst_ref=dst, send_sem=send, recv_sem=recv, device_id=device, device_id_type=MESH
        )

    def beside_copies(src, dst, slot, axis):
        place, count = (gx, ngx) if axis == 0 else (gy, ngy)
        higher = (gx + 1, gy) if axis == 0 else (gx, gy + 1)
        lower = (gx - 1, gy) if axis == 0 else (gx, gy - 1)
        up = far(src.at[0], dst.at[0], near_send.at[slot, 0], near_recv.at[slot, 0], higher)
        down = far(src.at[1], dst.at[1], near_send.at[slot, 1], near_recv.at[slot, 1], lower)
        return place, count, up, down

    def beside_start(src, dst, slot, axis):
        place, count, up, down = beside_copies(src, dst, slot, axis)

        @pl.when(place < count - 1)
        def _():
            up.start()

        @pl.when(place > 0)
        def _():
            down.start()

    def beside_wait(src, dst, slot, axis):
        place, count, up, down = beside_copies(src, dst, slot, axis)

        @pl.when(place < count - 1)
        def _():
            up.wait_send()
            down.wait_recv()

        @pl.when(place > 0)
        def _():
            down.wait_send()
            up.wait_recv()

    def all_start(src, dst, slot):
        for peer in peers:
            far(src(peer), dst.at[gy], all_send.at[slot], all_recv.at[slot], (gx, peer)).start()

    def all_wait(dst, slot):
        others = dst.at[pl.ds(0, ngy - 1)]
        far(others, others, all_send.at[slot], all_recv.at[slot], (gx, peers[0])).wait()

    far_count = ngy // 4
    place_a = gy // 4
    place_b = lax.rem(gy // 2, 2)
    place_c = lax.rem(gy, 2)

    def tree_slot(k):
        if isinstance(k, int):
            return (k % 2 * 2 + k // 2 % 2) * far_count + k // 4
        return (lax.rem(k, 2) * 2 + lax.rem(k // 2, 2)) * far_count + k // 4

    def tree_copies(stage):
        if stage == 0:
            copies = []
            for j in range(1, far_count):
                a = lax.rem(place_a + j, far_count)
                slot = tree_slot(gy)
                peer = a * 4 + place_b * 2 + place_c
                there = far_count - j
                copies.append(
                    (
                        far(coef_s, coef_r.at[slot], tree_send.at[j], tree_recv.at[j], (gx, peer)),
                        far(coef_s, coef_r.at[tree_slot(peer)], tree_send.at[j], tree_recv.at[there], (gx, peer)),
                    )
                )
            return copies
        if stage == 1:
            mine = coef_r.at[pl.ds((place_c * 2 + place_b) * far_count, far_count)]
            theirs = coef_r.at[pl.ds((place_c * 2 + 1 - place_b) * far_count, far_count)]
            peer = place_a * 4 + (1 - place_b) * 2 + place_c
        else:
            mine = coef_r.at[pl.ds(place_c * 2 * far_count, 2 * far_count)]
            theirs = coef_r.at[pl.ds((1 - place_c) * 2 * far_count, 2 * far_count)]
            peer = place_a * 4 + place_b * 2 + 1 - place_c
        slot = ngy + stage - 1
        return [
            (
                far(mine, mine, tree_send.at[slot], tree_recv.at[slot], (gx, peer)),
                far(mine, theirs, tree_send.at[slot], tree_recv.at[slot], (gx, peer)),
            )
        ]

    def tree_start(stage):
        for outgoing, incoming in tree_copies(stage):
            outgoing.start()

    def tree_wait(stage):
        for outgoing, incoming in tree_copies(stage):
            outgoing.wait_send()
            incoming.wait_recv()

    def side_start(src, dst, slot):
        for j in range(1, ngx):
            peer = lax.rem(gx + j, ngx)
            far(src, dst.at[gx], side_send.at[slot, j], side_recv.at[slot, gx], (peer, gy)).start()

    def side_wait(src, dst, slot):
        for j in range(1, ngx):
            peer = lax.rem(gx + j, ngx)
            far(src, dst.at[peer], side_send.at[slot, j], side_recv.at[slot, peer], (peer, gy)).wait()

    for ref in (rx, ry, xu_r, xv_r, h2_r):
        ref[...] = jnp.zeros_like(ref)
    barrier = pltpu.get_barrier_semaphore()

    for peer in peers:
        pl.semaphore_signal(barrier, inc=1, device_id=(gx, peer), device_id_type=MESH)
    for j in range(1, ngx):
        pl.semaphore_signal(barrier, inc=1, device_id=(lax.rem(gx + j, ngx), gy), device_id_type=MESH)
    for load in loads:
        load.wait()
    pl.semaphore_wait(barrier, ngy - 1 + ngx - 1)

    row = lax.broadcasted_iota(jnp.int32, (wide, lanes), 0)
    lane = lax.broadcasted_iota(jnp.int32, (wide, lanes), 1)
    opened = [jnp.where(mask[y] != 2, 1.0, 0.0) for y in range(rows)]
    for y in range(rows):
        sx[0, pl.ds(y, 1), :] = (cond_x[y] * opened[y])[wide - 1 :]
        sx[1, pl.ds(y, 1), :] = opened[y][:1]
    sy[0] = cond_y[rows - 1] * opened[rows - 1]
    sy[1] = opened[0]
    beside_start(sx, rx, 0, 0)
    beside_start(sy, ry, 1, 1)
    beside_wait(sx, rx, 0, 0)
    beside_wait(sy, ry, 1, 1)
    faces_y = []
    lows_y = [ry[0] * opened[0]]
    shifts = []
    for y in range(rows):
        now = opened[y]
        cx = cond_x[y] * now
        one["fx"][y] = cx * jnp.where(row == wide - 1, rx[1, pl.ds(y, 1), :], pltpu.roll(now, wide - 1, 0))
        one["lx"][y] = now * jnp.where(row == 0, rx[0, pl.ds(y, 1), :], pltpu.roll(cx, 1, 0))
        above = opened[y + 1] if y + 1 < rows else ry[1]
        faces_y.append(cond_y[y] * now * above)
        if y + 1 < rows:
            lows_y.append(faces_y[y])
        fz = cond_z[y] * now * jnp.where(lane == lanes - 1, 0.0, pltpu.roll(now, lanes - 1, 1))
        one["fz"][y] = fz
        one["lz"][y] = pltpu.roll(fz, 1, 1)
        shifts.append(base_shift + wall_term * jnp.where(mask[y] == 1, 1.0, 0.0))
        one["f"][y] = source[y] * now
    edge_fy[...] = faces_y[rows - 1]
    edge_ly[...] = lows_y[0]

    recs = []
    ratio = None
    for y in range(rows):
        diag = shifts[y] + one["fx"][y] + one["lx"][y] + faces_y[y] + lows_y[y] + one["fz"][y] + one["lz"][y]
        if y:
            diag = diag - lows_y[y] * ratio
        rec = 1.0 / diag
        ratio = faces_y[y] * rec
        recs.append(rec)
        one["rec"][y] = rec
        one["rat"][y] = ratio
        one["lr"][y] = lows_y[y] * rec

    def block_solve(right):
        value = right[0] * one["rec"][0]
        values = [value]
        for y in range(1, rows):
            value = right[y] * one["rec"][y] + one["lr"][y] * value
            values.append(value)
        for y in range(rows - 2, -1, -1):
            values[y] = values[y] + one["rat"][y] * values[y + 1]
        return values

    firsts = [recs[0]]
    for y in range(1, rows):
        firsts.append(one["lr"][y] * firsts[-1])
    lasts = [None] * (rows - 1) + [recs[rows - 1]]
    for y in range(rows - 2, -1, -1):
        firsts[y] = firsts[y] + one["rat"][y] * firsts[y + 1]
        lasts[y] = one["rat"][y] * lasts[y + 1]
    low, high = edge_ly[...], edge_fy[...]
    for y in range(rows):
        firsts[y] = low * firsts[y]
        lasts[y] = high * lasts[y]
        one["first"][y] = firsts[y]
        one["last"][y] = lasts[y]
    share = wide // ngy

    def shared(target, values):
        for place, value in enumerate(values):
            for owner in range(ngy):
                target[owner, place] = value[owner * share : (owner + 1) * share]

    def reduced(rhs, send):
        zero = jnp.zeros((share, lanes), jnp.float32)

        def down(k, carry):
            p = carry
            start = (rhs[k, 0] + face_r[k, 0] * p) * red[k, 1]
            terms[k, 0] = start
            terms[k, 1] = p
            return rhs[k, 1] + face_r[k, 2] * (p + red[k, 0] * start)

        def up(step, after):
            k = ngy - 1 - step
            first = terms[k, 0] + red[k, 2] * after
            send[k, 0] = terms[k, 1] + red[k, 0] * first
            send[k, 1] = after
            return first

        looped(ngy, down, zero, 16)
        looped(ngy, up, zero, 16)

    def reduced_factor():
        def step(k, q):
            inv = 1.0 / (1.0 - face_r[k, 0] * q)
            slope = face_r[k, 1] * inv
            red[k, 0] = q
            red[k, 1] = inv
            red[k, 2] = slope
            return face_r[k, 3] + face_r[k, 2] * q * slope

        looped(ngy, step, jnp.zeros((share, lanes), jnp.float32), 16)

    def joined(local, got):
        for owner in range(ngy):
            whole_prev[pl.ds(owner * share, share), :] = got[owner, 0]
            whole_next[pl.ds(owner * share, share), :] = got[owner, 1]
        prev, after = whole_prev[...], whole_next[...]
        return [local[y] + prev * one["first"][y] + after * one["last"][y] for y in range(rows)]

    local = block_solve([one["f"][y] for y in range(rows)])
    shared(face_s, [firsts[0], lasts[0], firsts[rows - 1], lasts[rows - 1], local[0], local[rows - 1]])
    face_r[gy] = face_s[gy]
    all_start(lambda peer: face_s.at[peer], face_r, 1)

    half = rows // 2
    quarter = rows // 4
    wide2 = wide // 2
    both = lanes // 2

    def packed(flat):
        whole = flat.reshape(half, wide2, lanes)
        return whole[:quarter] + pltpu.roll(whole[quarter:], both, 2)

    coarse_fx = coarsened(one["fx"][...], work, x_odd=True)
    coef_s[pl.ds(0, quarter)] = packed(coarse_fx)
    coef_s[pl.ds(quarter, quarter)] = packed(coarsened(jnp.stack(faces_y), work, y_odd=True))
    coef_s[pl.ds(2 * quarter, quarter)] = packed(coarsened(one["fz"][...], work, z_odd=True))
    coef_s[pl.ds(3 * quarter, quarter)] = packed(coarsened(jnp.stack(shifts), work))
    lx_all = one["lx"][...].reshape(half, 2, wide, lanes)
    lx_rows = (lx_all[:, 0] + lx_all[:, 1]).reshape(half * wide, lanes)
    work[pl.ds(0, half * wide), :] = times(lx_rows, pairing(None))
    for y in range(half):
        coef_s[4 * quarter, pl.ds(y, 1), :] = 0.25 * work[pl.ds(y * wide, 1), :]
    coef_r[tree_slot(gy)] = coef_s[...]
    tree_start(0)
    all_wait(face_r, 1)
    reduced_factor()
    reduced(face_r.at[:, pl.ds(4, 2)], back_s)
    back_r[gy] = back_s[gy]
    all_start(lambda peer: back_s.at[peer], back_r, 2)
    tree_wait(0)
    tree_start(1)
    all_wait(back_r, 2)
    values = joined(local, back_r)

    def outer_planes(values, target):
        for y in range(rows):
            target[0, pl.ds(y, 1), :] = values[y][wide - 1 :]
            target[1, pl.ds(y, 1), :] = values[y][:1]

    def beside_one(y, u, got):
        return (
            one["fx"][y] * jnp.where(row == wide - 1, got[1, pl.ds(y, 1), :], pltpu.roll(u, wide - 1, 0))
            + one["lx"][y] * jnp.where(row == 0, got[0, pl.ds(y, 1), :], pltpu.roll(u, 1, 0))
            + one["fz"][y] * pltpu.roll(u, lanes - 1, 1)
            + one["lz"][y] * pltpu.roll(u, 1, 1)
        )

    outer_planes(values, xu_s)
    beside_start(xu_s, xu_r, 2, 0)
    for y in range(rows):
        one["u"][y] = values[y]
    tree_wait(1)
    tree_start(2)
    beside_wait(xu_s, xu_r, 2, 0)
    left = jnp.stack([beside_one(y, values[y], xu_r) for y in range(rows)])
    rhs_s[...] = packed(coarsened(left, work))
    rhs_r[gy] = rhs_s[...]
    all_start(lambda peer: rhs_s, rhs_r, 3)

    two, three = levels[0], levels[1]
    used = lax.broadcasted_iota(jnp.int32, (wide2, lanes), 1) < both

    def unpack2(target, block, k):
        for y in range(quarter):
            pair = block(y)
            target[half * k + y] = jnp.where(used, pair, 0.0)
            target[half * k + quarter + y] = jnp.where(used, pltpu.roll(pair, both, 1), 0.0)

    tree_wait(2)

    def take_coefs(k, carry):
        for place, target in enumerate((two.fx, two.fy, two.fz, two.sh)):
            unpack2(target, lambda y: coef_r[tree_slot(k), place * quarter + y], k)
        return carry

    for k in range(ngy):
        take_coefs(k, 0)

    rows3 = three.rows
    part3 = rows3 // 4
    wide3 = wide2 // 2
    step3 = lanes // 4

    def packed3(flat):
        whole = flat.reshape(rows3, wide3, lanes)
        total = whole[:part3]
        for j in range(1, 4):
            total = total + pltpu.roll(whole[j * part3 : (j + 1) * part3], j * step3, 2)
        return total

    used3 = lax.broadcasted_iota(jnp.int32, (part3, wide3, lanes), 2) < step3

    def unpack3(target, got):
        for g in range(ngx):
            block = got(g)
            for j in range(4):
                turned = block if j == 0 else pltpu.roll(block, lanes - j * step3, 2)
                target[pl.ds(j * part3, part3), pl.ds(g * wide3, wide3), :] = jnp.where(used3, turned, 0.0)

    c3_s[0] = packed3(coarsened(two.fx[...], work, x_odd=True))
    c3_s[1] = packed3(coarsened(two.fy[...], work, y_odd=True))
    c3_s[2] = packed3(coarsened(two.fz[...], work, z_odd=True))
    c3_s[3] = packed3(coarsened(two.sh[...], work))
    c3_r[gx] = c3_s[...]
    side_start(c3_s, c3_r, 0)

    def edge2(y):
        return h2_s[0, pl.ds(y, 1), :]

    def take_edges(k, carry):
        for y in range(half):
            h2_s[0, pl.ds(half * k + y, 1), :] = coef_r[tree_slot(k), 4 * quarter, pl.ds(y, 1), :]
        return carry

    for k in range(ngy):
        take_edges(k, 0)
    two.factor(edge2)
    all_wait(rhs_r, 3)

    def take_rhs(k, carry):
        unpack2(two.g, lambda y: rhs_r[k, y], k)
        return carry

    for k in range(ngy):
        take_rhs(k, 0)
    two.solve(False)

    def outer_two(target):
        def step(y, carry):
            target[0, pl.ds(y, 1), :] = two.u[y, pl.ds(wide2 - 1, 1), :]
            target[1, pl.ds(y, 1), :] = two.u[y, pl.ds(0, 1), :]
            return carry

        looped(two.rows, step, 0, 16)

    outer_two(h2_s)
    beside_start(h2_s, h2_r, 3, 0)
    side_wait(c3_s, c3_r, 0)
    for place, target in enumerate((three.fx, three.fy, three.fz, three.sh)):
        unpack3(target, lambda g: c3_r[g, place])
    for fine, level in zip(levels[1:], levels[2:]):
        put_rows(level.fx, coarsened(fine.fx[...], work, x_odd=True), level.rows)
        put_rows(level.fy, coarsened(fine.fy[...], work, y_odd=True), level.rows)
        put_rows(level.fz, coarsened(fine.fz[...], work, z_odd=True), level.rows)
        put_rows(level.sh, coarsened(fine.sh[...], work), level.rows)
    for level in levels[1:]:
        level.factor()
    beside_wait(h2_s, h2_r, 3, 0)
    two.halo = h2_r
    two.residual(hold)
    g3_s[...] = packed3(coarsened(hold[...], work, y_summed=True))
    g3_r[gx] = g3_s[...]
    side_start(g3_s, g3_r, 1)
    side_wait(g3_s, g3_r, 1)
    unpack3(three.g, lambda g: g3_r[g])
    for fine, level in zip(levels[1:], levels[2:]):
        fine.solve(False)
        part = hold.at[pl.ds(0, fine.rows // 2), pl.ds(0, fine.wide)]
        fine.residual(part)
        put_rows(level.g, coarsened(part[...], work, y_summed=True), level.rows)
    levels[-1].solve(False)
    levels[-1].solve(True)
    for fine, level in zip(levels[-2:0:-1], levels[:1:-1]):
        spread_add(fine.u, level.u[...], fine.wide, work)
        fine.solve(True)
    spread_add(two.u, three.u[:, pl.ds(pl.multiple_of(gx * wide3, 8), wide3), :], wide2, work)
    for side, plane in enumerate((lax.max(gx * wide3 - 1, 0), lax.min((gx + 1) * wide3, three.width - 1))):

        def pick(y, carry):
            work[pl.ds(y, 1), :] = three.u[y, pl.ds(plane, 1), :]
            return carry

        looped(rows3, pick, 0, 16)
        extra = times(work[pl.ds(0, rows3), :], spreading())
        work[pl.ds(0, rows3, stride=2), :] = extra
        work[pl.ds(1, rows3, stride=2), :] = extra
        h2_r[side] = h2_r[side] + work[pl.ds(0, 2 * rows3), :]
    two.solve(True)
    spread_add(one["u"], two.u[pl.ds(gy * half, half)], wide, work)
    values = [one["u"][y] for y in range(rows)]
    outer_planes(values, xv_s)
    beside_start(xv_s, xv_r, 5, 0)
    beside_wait(xv_s, xv_r, 5, 0)
    local = block_solve([one["f"][y] + beside_one(y, values[y], xv_r) for y in range(rows)])
    shared(face2_s, [local[0], local[rows - 1]])
    face2_r[gy] = face2_s[gy]
    all_start(lambda peer: face2_s.at[peer], face2_r, 4)
    all_wait(face2_r, 4)
    reduced(face2_r, back2_s)
    back2_r[gy] = back2_s[gy]
    all_start(lambda peer: back2_s.at[peer], back2_r, 5)
    all_wait(back2_r, 5)
    values = joined(local, back2_r)
    for y in range(rows):
        out[y] = values[y]


def fused(ngx, ngy, *args):
    rows, wide, lanes = args[0].shape
    f32 = jnp.float32
    levels = [Coarse(rows // 2 * ngy, wide // 2, lanes // 2)]
    for depth in range(2, LEVELS):
        whole = wide * ngx >> depth
        levels.append(Coarse(rows * ngy >> depth, whole, lanes >> depth))
    two, three = levels[:2]
    share = wide // ngy
    quarter = rows // 4
    wide2 = wide // 2

    def room(*shape):
        return pltpu.VMEM(shape, f32)

    part3 = three.rows // 4
    wide3 = wide2 // 2
    most = max(rows * wide, two.rows * two.wide, three.rows * three.wide)
    scratch = [pltpu.VMEM(arg.shape, arg.dtype) for arg in args]
    scratch += [room(most, lanes), room(two.rows // 2, two.wide, lanes)]
    scratch += [room(rows, wide, lanes)] * 11
    scratch += [room(wide, lanes)] * 2
    scratch += [room(2, rows, lanes)] * 2 + [room(2, wide, lanes)] * 2
    count = 4 * quarter + 1
    scratch += [room(count, wide2, lanes), room(ngy, count, wide2, lanes)]
    scratch += [room(quarter, wide2, lanes), room(ngy, quarter, wide2, lanes)]
    scratch += [room(ngy, 6, share, lanes)] * 2 + [room(ngy, 2, share, lanes)] * 6
    scratch += [room(ngy, 3, share, lanes), room(ngy, 2, share, lanes)]
    scratch += [room(wide, lanes)] * 2
    scratch += [room(2, rows, lanes)] * 4 + [room(2, two.rows, lanes)] * 2
    scratch += [room(4, part3, wide3, lanes), room(ngx, 4, part3, wide3, lanes)]
    scratch += [room(part3, wide3, lanes), room(ngx, part3, wide3, lanes)]
    for level in levels:
        scratch += level.scratch()
    dma = pltpu.SemaphoreType.DMA
    scratch += [dma((6, 2)), dma((6, 2)), dma((6,)), dma((6,)), dma((2, ngx)), dma((2, ngx)), dma((5,))]
    scratch += [dma((ngy + 2,)), dma((ngy + 2,))]
    return pl.pallas_call(
        functools.partial(v_cycle_kernel, ngx, ngy, levels),
        out_shape=jax.ShapeDtypeStruct(args[0].shape, f32),
        in_specs=[pl.BlockSpec(memory_space=pltpu.HBM)] * 5,
        out_specs=pl.BlockSpec(memory_space=pltpu.VMEM),
        scratch_shapes=scratch,
        compiler_params=pltpu.CompilerParams(
            collective_id=0, has_side_effects=True, vmem_limit_bytes=63 * 2**20
        ),
    )(*args)


def solution(mesh):
    ngx, ngy = mesh.shape["gx"], mesh.shape["gy"]
    small = ngy == 16 and ngx <= 4
    part = functools.partial(fused, ngx, ngy) if small else body
    return jax.shard_map(
        part,
        mesh=mesh,
        in_specs=(P("gy", "gx", None),) * 5,
        out_specs=P("gy", "gx", None),
        check_vma=False,
    )
```
